256 devices in a mesh: kvseq: 32 (over z, y), head: 8 (over x, core).
Axes of the slice: x: 4, y: 4, z: 8, core: 2. Of those that a mesh axis runs over, the one named last changes fastest.
Arguments:
- lengths: int32 [4], replicated, may hold values from 16 to 65536, as said below
- queries: bfloat16 [4, 16, 8192], P(None, None, 'head'), may hold values from -8 to 8
- cache_keys: bfloat16 [4, 65536, 1024], P(None, 'kvseq', 'head'), may hold values from -8 to 8
- cache_values: bfloat16 [4, 65536, 1024], P(None, 'kvseq', 'head'), may hold values from -8 to 8
- residual_in: bfloat16 [64, 8192], P(None, ('kvseq', 'head')), may hold values from -24 to 24
- out_weight: bfloat16 [8192, 8192], P('head', 'kvseq'), may hold values from -0.0625 to 0.0625
- norm_gain: bfloat16 [8192], P(('kvseq', 'head')), may hold values from 0.099609375 to 1.8984375
- gate_weight: bfloat16 [8192, 28672], P(None, ('kvseq', 'head')), may hold values from -0.25 to 0.25
- up_weight: bfloat16 [8192, 28672], P(None, ('kvseq', 'head')), may hold values from -0.25 to 0.25
- down_weight: bfloat16 [28672, 8192], P(('kvseq', 'head')), may hold values from -0.15625 to 0.15625
Outputs:
- layer_out: bfloat16 [64, 8192], P(None, ('kvseq', 'head'))
The draws below stay inside these ranges and needn't reach their ends.
Inputs may be any that keep to these rules, and one draw needn't show every extreme that they name: `lengths`: every sequence holds at least its 16 new tokens; some sequence fills the whole cache of 65536 positions.
All inputs are finite; a program needn't handle non-finite values.
Results may differ from the reference program's by a relative error of at most 0.015.
Values may be sent and summed in bfloat16 or wider, within the bound.
No kernel may reach another device: no remote copies, remote signals or barrier semaphores. Data moves between devices by JAX's collectives and lax.ppermute only.
A program may use at most 128 MiB of HBM per device.

```python
import math
import jax
import jax.numpy as jnp
from jax import lax

D = 8192
FF = 28672
HQ = 64
KVH = 8
HD = 128
ROWS = 4
DRAFTS = 16
SEQ = 65536
TOKENS = 64


def draw_lengths(key, part):
    key = jax.random.fold_in(key, 5)
    first_key, second_key = jax.random.split(key)
    picked = jax.random.randint(first_key, (ROWS,), DRAFTS, SEQ + 1)
    longest = jax.random.randint(second_key, (), 0, ROWS)
    return jnp.where(jnp.arange(ROWS) == longest, SEQ, picked).astype(jnp.int32)


def draw_queries(key, part):
    key = jax.random.fold_in(key, 1)
    field_base = jax.random.truncated_normal(key, -6.0, 6.0, (ROWS, DRAFTS, HQ * HD), jnp.float32)
    return field_base.astype(jnp.bfloat16)


def draw_cache_keys(key, part):
    key = jax.random.fold_in(key, 2)
    field_base = jax.random.truncated_normal(key, -6.0, 6.0, (ROWS, SEQ, KVH * HD), jnp.float32)
    return field_base.astype(jnp.bfloat16)


def draw_cache_values(key, part):
    key = jax.random.fold_in(key, 3)
    phase_key, noise_key = jax.random.split(key)
    phases = jax.random.uniform(phase_key, (1, 1, KVH * HD), jnp.float32, 0.0, 2.0 * math.pi)
    places = jnp.arange(SEQ, dtype=jnp.float32)[None, :, None] / SEQ
    smooth = 2.0 * jnp.sin(2.0 * math.pi * 3.0 * places + phases)
    noise = jax.random.truncated_normal(noise_key, -4.0, 4.0, (ROWS, SEQ, KVH * HD), jnp.float32)
    return (smooth + noise).astype(jnp.bfloat16)


def draw_residual_in(key, part):
    key = jax.random.fold_in(key, 4)
    noise_key = jax.random.fold_in(key, 0)
    column_scale = 1.0 + 2.0 * jnp.arange(D, dtype=jnp.float32)[None, :] / (D - 1)
    noise = jax.random.truncated_normal(noise_key, -4.0, 4.0, (TOKENS, D), jnp.float32)
    return (noise * column_scale).astype(jnp.bfloat16)


def strengthened(drawn, key, source, target, shards_of, factor):
    owner, partner = [(jnp.arange(drawn.shape[dim]) // (drawn.shape[dim] // shards_of)).reshape([-1 if axis == dim else 1 for axis in range(drawn.ndim)]) for dim in (source, target)]
    chosen = jax.random.permutation(key, shards_of)[partner]
    strong = (owner == chosen) | (owner == (partner + shards_of // 2) % shards_of)
    return jnp.where(strong, factor * drawn, drawn)


def steps_of(rng, extent, cuts, least, high):
    level, own = 1.0, jax.random.fold_in(rng, 6)
    for position, shards_of in cuts:
        steps = jnp.exp(jax.random.uniform(jax.random.fold_in(own, position), (shards_of,), jnp.float32, least / len(cuts), high / len(cuts)))
        level = level * jnp.repeat(steps, extent[position] // shards_of).reshape([-1 if axis == position else 1 for axis in range(len(extent))])
    return level


def gaussian(own_key, extent, width, limit, cuts=(), kind=jnp.bfloat16):
    result = jax.random.normal(own_key, extent, jnp.float32) * width
    if len(cuts) > 0:
        result = steps_of(own_key, extent, cuts, -0.22, 0.18) * result
    return jnp.clip(result, min=-limit, max=limit).astype(kind)


def noise_with(key, shape, width, most, pieces, heavy, kind=jnp.bfloat16):
    entries = width * jax.random.normal(key, shape, jnp.float32)
    if pieces:
        entries = entries * steps_of(key, shape, pieces, -0.22, 0.18)
    return jnp.clip(strengthened(entries, jax.random.fold_in(key, 3), *heavy), -most, most).astype(kind)


def setup_inputs(seed: int = 0) -> dict:
    key_list = jax.random.split(jax.random.key(seed), 11)
    lengths = draw_lengths(jax.random.fold_in(key_list[10], 71), 0)
    queries = draw_queries(jax.random.fold_in(key_list[10], 71), 0)
    cache_keys = draw_cache_keys(jax.random.fold_in(key_list[10], 71), 0)
    cache_values = draw_cache_values(jax.random.fold_in(key_list[10], 71), 0)
    residual_in = draw_residual_in(jax.random.fold_in(key_list[10], 71), 0)
    out_weight = gaussian(key_list[5], (HQ * HD, D), (HQ * HD) ** -0.5, 0.0625, ((0, 8), (1, 32)))
    norm_gain = jnp.clip(1.0 + 0.18 * jax.random.normal(key_list[6], (D,), jnp.float32), 0.099609375, 1.8984375).astype(jnp.bfloat16)
    gate_weight = noise_with(key_list[7], (D, FF), D ** -0.5, 0.25, ((1, 256),), (0, 1, 256, 6.0))
    up_weight = noise_with(key_list[8], (D, FF), D ** -0.5, 0.25, ((1, 256),), (0, 1, 256, 6.0))
    down_weight = noise_with(key_list[9], (FF, D), FF ** -0.5, 0.15625, ((0, 256),), (0, 1, 256, 6.0))
    return {"lengths": lengths, "queries": queries, "cache_keys": cache_keys, "cache_values": cache_values, "residual_in": residual_in, "out_weight": out_weight, "norm_gain": norm_gain, "gate_weight": gate_weight, "up_weight": up_weight, "down_weight": down_weight}


NEG_FILL = -1e+30
EPSILON = 1e-05

def attend_pair(pair, lengths, queries, cache_keys, cache_values):
    group_size = HQ // KVH
    row_index = (pair // KVH).astype(jnp.int32)
    kv_head = (pair % KVH).astype(jnp.int32)
    query_row = lax.dynamic_index_in_dim(queries, row_index, 0, keepdims=False)
    key_row = lax.dynamic_index_in_dim(cache_keys, row_index, 0, keepdims=False)
    value_row = lax.dynamic_index_in_dim(cache_values, row_index, 0, keepdims=False)
    query_block = lax.dynamic_slice_in_dim(query_row, (kv_head * group_size * HD).astype(jnp.int32), group_size * HD, 1)
    query_mat = query_block.reshape(DRAFTS, group_size, HD).transpose(1, 0, 2).reshape(group_size * DRAFTS, HD)
    key_mat = lax.dynamic_slice_in_dim(key_row, (kv_head * HD).astype(jnp.int32), HD, 1)
    value_mat = lax.dynamic_slice_in_dim(value_row, (kv_head * HD).astype(jnp.int32), HD, 1)
    scores = jnp.dot(query_mat, key_mat.T, preferred_element_type=jnp.float32) * (1.0 / math.sqrt(HD))
    length = lax.dynamic_index_in_dim(lengths, row_index, 0, keepdims=False)
    positions = length - DRAFTS + jnp.arange(DRAFTS, dtype=jnp.int32)
    positions = jnp.tile(positions, group_size)
    visible = jnp.arange(SEQ, dtype=jnp.int32)[None, :] <= positions[:, None]
    masked = jnp.where(visible, scores, NEG_FILL)
    largest = lax.optimization_barrier(jnp.max(masked, axis=1))
    weights = jnp.where(visible, jnp.exp(masked - largest[:, None]), 0.0)
    total = lax.optimization_barrier(jnp.sum(weights, axis=1))
    weighted = jnp.dot(weights.astype(jnp.bfloat16), value_mat, preferred_element_type=jnp.float32)
    return (weighted / total[:, None]).reshape(group_size, DRAFTS, HD)

def reference(lengths, queries, cache_keys, cache_values, residual_in, out_weight, norm_gain, gate_weight, up_weight, down_weight):
    group_size = HQ // KVH
    pairs = jnp.arange(ROWS * KVH, dtype=jnp.int32)
    heads_out = lax.map(lambda pair: attend_pair(pair, lengths, queries, cache_keys, cache_values), pairs)
    heads_out = heads_out.reshape(ROWS, KVH, group_size, DRAFTS, HD).transpose(0, 3, 1, 2, 4)
    attn = heads_out.reshape(TOKENS, HQ * HD).astype(jnp.bfloat16)
    projected = jnp.dot(attn, out_weight, preferred_element_type=jnp.float32)
    mixed = (residual_in.astype(jnp.float32) + projected).astype(jnp.bfloat16)
    mixed_wide = mixed.astype(jnp.float32)
    mean_square = lax.optimization_barrier(jnp.mean(mixed_wide * mixed_wide, axis=1))
    normed = (mixed_wide * lax.rsqrt(mean_square + EPSILON)[:, None] * norm_gain.astype(jnp.float32)[None, :]).astype(jnp.bfloat16)
    gate = jnp.dot(normed, gate_weight, preferred_element_type=jnp.float32)
    upward = jnp.dot(normed, up_weight, preferred_element_type=jnp.float32)
    hidden = (jax.nn.silu(gate) * upward).astype(jnp.bfloat16)
    ffn_term = jnp.dot(hidden, down_weight, preferred_element_type=jnp.float32)
    return (mixed_wide + ffn_term).astype(jnp.bfloat16)
```

```python
import functools
import math

import jax
import jax.numpy as jnp
from jax import lax
from jax.experimental import pallas as pl
from jax.experimental.pallas import tpu as pltpu
from jax.sharding import Mesh, PartitionSpec as P

D = 8192
FF = 28672
HD = 128
GROUP = 8
ROWS = 4
DRAFTS = 16
TOKENS = 64
KV = 32
SLICE = 2048
CHUNK = 512
NEG = -1e30
FLOOR = -1e29
EPSILON = 1e-05
LOG_SCALE = math.log2(math.e) / math.sqrt(HD)
MIB = 1024 * 1024
F32 = jnp.float32
BF16 = jnp.bfloat16
VMEM = pl.BlockSpec(memory_space=pltpu.VMEM)
SMEM = pl.BlockSpec(memory_space=pltpu.SMEM)


def nt(a, b):
    return lax.dot_general(a, b, (((1,), (1,)), ((), ())), preferred_element_type=F32)


def nn(a, b):
    return jnp.dot(a, b, preferred_element_type=F32)


def lanes(shape):
    return lax.broadcasted_iota(jnp.int32, shape, len(shape) - 1)


def attend(place_ref, lengths_ref, gain_ref, q_ref, k_ref, v_ref, out_ref, score_ref):
    row = pl.program_id(0)
    first_key = place_ref[0] * SLICE
    length = lengths_ref[row]
    queries = jnp.concatenate(
        [q_ref[0, :, g * HD : (g + 1) * HD] for g in range(GROUP)], axis=0
    )
    draft = lax.broadcasted_iota(jnp.int32, (GROUP * DRAFTS, CHUNK), 0) % DRAFTS
    limit = length - DRAFTS + draft - first_key - lanes((GROUP * DRAFTS, CHUNK))
    peak = jnp.full((GROUP * DRAFTS, HD), NEG, F32)
    for n in range(SLICE // CHUNK):
        scores = nt(queries, k_ref[0, n * CHUNK : (n + 1) * CHUNK, :]) * LOG_SCALE
        scores = jnp.where(limit >= n * CHUNK, scores, NEG)
        score_ref[:, n * CHUNK : (n + 1) * CHUNK] = scores
        for i in range(CHUNK // HD):
            peak = jnp.maximum(peak, scores[:, i * HD : (i + 1) * HD])
    top = jnp.max(peak, axis=1, keepdims=True).astype(BF16).astype(F32)
    base = jnp.maximum(top, FLOOR)
    acc = jnp.zeros((GROUP * DRAFTS, HD), F32)
    sums = jnp.zeros((GROUP * DRAFTS, HD), F32)
    for n in range(SLICE // CHUNK):
        weights = jnp.exp2(score_ref[:, n * CHUNK : (n + 1) * CHUNK] - base)
        for i in range(CHUNK // HD):
            sums = sums + weights[:, i * HD : (i + 1) * HD]
        acc = acc + nn(weights.astype(BF16), v_ref[0, n * CHUNK : (n + 1) * CHUNK, :])
    total = jnp.sum(sums, axis=1, keepdims=True)
    lane = lanes((GROUP * DRAFTS, HD))
    gain = jnp.broadcast_to(gain_ref[...].astype(F32), (GROUP * DRAFTS, HD))
    stats = jnp.where(lane < 32, top, jnp.where(lane < 64, total, gain))
    out_ref[:, 0:16, :] = acc.astype(BF16).reshape(GROUP, DRAFTS, HD)
    out_ref[:, 16:32, :] = stats.astype(BF16).reshape(GROUP, DRAFTS, HD)


def attention(place, lengths, gain_row, queries, keys, values):
    return pl.pallas_call(
        attend,
        grid=(ROWS,),
        in_specs=[
            SMEM,
            SMEM,
            pl.BlockSpec((1, HD), lambda r: (0, 0)),
            pl.BlockSpec((1, DRAFTS, GROUP * HD), lambda r: (r, 0, 0)),
            pl.BlockSpec((1, SLICE, HD), lambda r: (r, 0, 0)),
            pl.BlockSpec((1, SLICE, HD), lambda r: (r, 0, 0)),
        ],
        out_specs=pl.BlockSpec((GROUP, 32, HD), lambda r: (r, 0, 0)),
        out_shape=jax.ShapeDtypeStruct((KV, 32, HD), BF16),
        scratch_shapes=[pltpu.VMEM((GROUP * DRAFTS, SLICE), F32)],
        compiler_params=pltpu.CompilerParams(vmem_limit_bytes=16 * MIB),
        name="attention",
    )(place, lengths, gain_row, queries, keys, values)


def combine(in_ref, attn_ref, gain_ref):
    top = in_ref[:, 16:32, 0:1].astype(F32)
    total = in_ref[:, 16:32, 32:33].astype(F32)
    joint = jnp.max(top, axis=0, keepdims=True)
    factor = jnp.exp2(top - joint)
    whole = jnp.sum(total * factor, axis=0)
    acc = jnp.sum(in_ref[:, 0:16, :].astype(F32) * factor, axis=0)
    attn = (acc / whole).astype(BF16)
    attn_ref[...] = jnp.broadcast_to(attn[None], (KV, DRAFTS, HD))
    pick = lanes((KV, KV * 16)) == 16 * lax.broadcasted_iota(jnp.int32, (KV, KV * 16), 0)
    stats = in_ref[:, 16:32, :].reshape(KV * 16, HD)
    gain_ref[...] = nn(pick.astype(F32).astype(BF16), stats).astype(BF16)


def combined(parts):
    return pl.pallas_call(
        combine,
        in_specs=[VMEM],
        out_specs=[VMEM, VMEM],
        out_shape=[
            jax.ShapeDtypeStruct((KV, DRAFTS, HD), BF16),
            jax.ShapeDtypeStruct((KV, HD), BF16),
        ],
        compiler_params=pltpu.CompilerParams(vmem_limit_bytes=16 * MIB),
        name="combine",
    )(parts)


def project(place_ref, attn_ref, weight_ref, residual_ref, gain_ref, own_ref, other_ref):
    core = place_ref[2]
    head = place_ref[1] * 2 + core
    attn = jnp.concatenate(
        [
            jnp.concatenate([attn_ref[r * GROUP + g] for g in range(GROUP)], axis=1)
            for r in range(ROWS)
        ],
        axis=0,
    )
    spread = nn(attn, weight_ref[...])
    source = lax.broadcasted_iota(jnp.int32, (32, 256), 0)
    put = (lanes((32, 256)) == head * 32 + source).astype(F32).astype(BF16)
    spread = spread + nn(residual_ref[...], put)
    source = lax.broadcasted_iota(jnp.int32, (HD, 256), 0)
    put = ((lanes((HD, 256)) == head * 32 + source - 64) & (source >= 64) & (source < 96))
    gain = nn(gain_ref[...], put.astype(F32).astype(BF16))
    both = jnp.concatenate([spread, gain], axis=0)
    own_ref[...] = jnp.where(core == 0, both[:, :HD], both[:, HD:])
    other_ref[...] = jnp.where(core == 0, both[:, HD:], both[:, :HD]).astype(BF16)


def projected(place, attn, weight, residual, gain):
    return pl.pallas_call(
        project,
        in_specs=[SMEM, VMEM, VMEM, VMEM, VMEM],
        out_specs=[VMEM, VMEM],
        out_shape=[
            jax.ShapeDtypeStruct((TOKENS + KV, HD), F32),
            jax.ShapeDtypeStruct((TOKENS + KV, HD), BF16),
        ],
        compiler_params=pltpu.CompilerParams(vmem_limit_bytes=16 * MIB),
        name="project",
    )(place, attn, weight, residual, gain)


def mix(a_ref, b_ref, c_ref, d_ref, mixed_ref, gain_ref):
    total = (a_ref[...].astype(F32) + b_ref[...].astype(F32)) + (
        c_ref[...].astype(F32) + d_ref[...].astype(F32)
    )
    mixed = total[:TOKENS].astype(BF16)
    mixed_ref[...] = jnp.broadcast_to(mixed[None], (KV, TOKENS, HD))
    gain_ref[...] = total[TOKENS:].astype(BF16)


def mixing(parts):
    return pl.pallas_call(
        mix,
        in_specs=[VMEM] * 4,
        out_specs=[VMEM, VMEM],
        out_shape=[
            jax.ShapeDtypeStruct((KV, TOKENS, HD), BF16),
            jax.ShapeDtypeStruct((KV, HD), BF16),
        ],
        compiler_params=pltpu.CompilerParams(vmem_limit_bytes=16 * MIB),
        name="mix",
    )(*parts)


def feed(
    place_ref, own_ref, other_ref, own_gain_ref, other_gain_ref,
    gate_ref, up_ref, down_ref, own_out_ref, other_out_ref,
):
    core = place_ref[2]
    squares = jnp.zeros((TOKENS, HD), F32)
    for k in range(KV):
        a = own_ref[k].astype(F32)
        b = other_ref[k].astype(F32)
        squares = squares + a * a + b * b
    scale = lax.rsqrt(jnp.sum(squares, axis=1, keepdims=True) / D + EPSILON)
    gate = jnp.zeros((TOKENS, gate_ref.shape[1]), F32)
    upward = jnp.zeros((TOKENS, gate_ref.shape[1]), F32)
    for k in range(KV):
        a = own_ref[k].astype(F32) * scale * own_gain_ref[k : k + 1, :].astype(F32)
        b = other_ref[k].astype(F32) * scale * other_gain_ref[k : k + 1, :].astype(F32)
        left = jnp.where(core == 0, a, b)
        right = jnp.where(core == 0, b, a)
        normed = jnp.concatenate([left, right], axis=1).astype(BF16)
        gate = gate + nn(normed, gate_ref[k * 256 : (k + 1) * 256, :])
        upward = upward + nn(normed, up_ref[k * 256 : (k + 1) * 256, :])
    hidden = (gate / (1.0 + jnp.exp(-gate)) * upward).astype(BF16)
    for k in range(KV):
        terms = nn(hidden, down_ref[:, k * 256 : (k + 1) * 256]).astype(BF16)
        own_out_ref[k] = jnp.where(core == 0, terms[:, :HD], terms[:, HD:])
        other_out_ref[k] = jnp.where(core == 0, terms[:, HD:], terms[:, :HD])


def feeding(place, own, other, own_gain, other_gain, gate_weight, up_weight, down_weight):
    shape = jax.ShapeDtypeStruct((KV, TOKENS, HD), BF16)
    return pl.pallas_call(
        feed,
        in_specs=[SMEM] + [VMEM] * 7,
        out_specs=[VMEM, VMEM],
        out_shape=[shape, shape],
        compiler_params=pltpu.CompilerParams(vmem_limit_bytes=32 * MIB),
        name="feed",
    )(place, own, other, own_gain, other_gain, gate_weight, up_weight, down_weight)


def gather_sum(in_ref, out_ref):
    total = in_ref[0].astype(F32)
    for k in range(1, KV):
        total = total + in_ref[k].astype(F32)
    out_ref[...] = jnp.broadcast_to(total.astype(BF16)[None], (8, TOKENS, HD))


def summed(parts):
    return pl.pallas_call(
        gather_sum,
        in_specs=[VMEM],
        out_specs=VMEM,
        out_shape=jax.ShapeDtypeStruct((8, TOKENS, HD), BF16),
        compiler_params=pltpu.CompilerParams(vmem_limit_bytes=16 * MIB),
        name="gather_sum",
    )(parts)


def finish(place_ref, parts_ref, own_ref, other_ref, out_ref):
    kv, x, core = place_ref[0], place_ref[1], place_ref[2]
    half = x // 2
    total = jnp.zeros((TOKENS, HD), F32)
    for i in range(4):
        total = total + parts_ref[2 * i + half].astype(F32)
    mixed = jnp.where(half == core, own_ref[kv].astype(F32), other_ref[kv].astype(F32))
    both = mixed + total
    which = (x * 2 + core) % 4
    out = both[:, 0:32]
    for i in range(1, 4):
        out = jnp.where(which == i, both[:, i * 32 : (i + 1) * 32], out)
    out_ref[...] = out.astype(BF16)


def finished(place, parts, own, other):
    return pl.pallas_call(
        finish,
        in_specs=[SMEM] + [VMEM] * 3,
        out_specs=VMEM,
        out_shape=jax.ShapeDtypeStruct((TOKENS, 32), BF16),
        compiler_params=pltpu.CompilerParams(vmem_limit_bytes=16 * MIB),
        name="finish",
    )(place, parts, own, other)


SWAP = [(0, 1), (1, 0)]


def exchange(parts, axes):
    return lax.all_to_all(parts, axes, 0, 0, tiled=True)


def shards(
    lengths,
    queries,
    cache_keys,
    cache_values,
    residual_in,
    out_weight,
    norm_gain,
    gate_weight,
    up_weight,
    down_weight,
):
    place = jnp.stack(
        [lax.axis_index(("z", "y")), lax.axis_index("x"), lax.axis_index("c")]
    ).astype(jnp.int32)
    gain_row = jnp.tile(norm_gain, 4).reshape(1, HD)
    parts = attention(place, lengths, gain_row, queries, cache_keys, cache_values)
    attn, gain = combined(exchange(parts, ("z", "y")))
    attn = exchange(attn, ("z", "y"))
    own, other = projected(place, attn, out_weight, residual_in, gain)
    pair = (own + lax.ppermute(other, "c", SWAP).astype(F32)).astype(BF16)
    around = [lax.ppermute(pair, "x", [(i, (i + s) % 4) for i in range(4)]) for s in (1, 2, 3)]
    mixed, own_gain = mixing([pair] + around)
    other_gain = lax.ppermute(own_gain, "c", SWAP)
    own_mixed = exchange(mixed, ("z", "y"))
    other_mixed = lax.ppermute(own_mixed, "c", SWAP)
    own_terms, other_terms = feeding(
        place, own_mixed, other_mixed, own_gain, other_gain, gate_weight, up_weight, down_weight
    )
    terms = own_terms.astype(F32) + lax.ppermute(other_terms, "c", SWAP).astype(F32)
    terms = summed(exchange(terms.astype(BF16), ("z", "y")))
    return finished(place, exchange(terms, ("x", "c")), own_mixed, other_mixed)


def solution(mesh):
    fine = Mesh(mesh.devices.reshape(8, 4, 4, 2), ("z", "y", "x", "c"))
    kvseq, head = ("z", "y"), ("x", "c")
    every = kvseq + head
    placed = (
        P(),
        P(None, None, head),
        P(None, kvseq, head),
        P(None, kvseq, head),
        P(None, every),
        P(head, kvseq),
        P(every),
        P(None, every),
        P(None, every),
        P(every, None),
    )
    return jax.shard_map(
        shards, mesh=fine, in_specs=placed, out_specs=P(None, every), check_vma=False
    )
```

```python
import math

import jax
import jax.numpy as jnp
from jax import lax
from jax.experimental import pallas as pl
from jax.experimental.pallas import tpu as pltpu
from jax.sharding import Mesh, PartitionSpec as P

D = 8192
FF = 28672
HD = 128
GROUP = 8
ROWS = 4
DRAFTS = 16
TOKENS = 64
KV = 32
SLICE = 2048
CHUNK = 512
NEG = -1e30
FLOOR = -1e29
EPSILON = 1e-05
LOG_SCALE = math.log2(math.e) / math.sqrt(HD)
MIB = 1024 * 1024
F32 = jnp.float32
BF16 = jnp.bfloat16
VMEM = pl.BlockSpec(memory_space=pltpu.VMEM)
SMEM = pl.BlockSpec(memory_space=pltpu.SMEM)


def nt(a, b):
    return lax.dot_general(a, b, (((1,), (1,)), ((), ())), preferred_element_type=F32)


def nn(a, b):
    return jnp.dot(a, b, preferred_element_type=F32)


def tn(a, b):
    return lax.dot_general(a, b, (((0,), (0,)), ((), ())), preferred_element_type=F32)


def lanes(shape):
    return lax.broadcasted_iota(jnp.int32, shape, len(shape) - 1)


def attend(lengths_ref, gain_ref, q_ref, k_ref, v_ref, out_ref, score_ref):
    row = pl.program_id(0)
    first_key = (lax.axis_index("z") * 4 + lax.axis_index("y")) * SLICE
    length = lengths_ref[row]
    queries = jnp.concatenate(
        [q_ref[0, :, g * HD : (g + 1) * HD] for g in range(GROUP)], axis=0
    )
    draft = lax.broadcasted_iota(jnp.int32, (GROUP * DRAFTS, CHUNK), 0) % DRAFTS
    limit = length - DRAFTS + draft - first_key - lanes((GROUP * DRAFTS, CHUNK))
    peak = jnp.full((GROUP * DRAFTS, HD), NEG, F32)
    for n in range(SLICE // CHUNK):
        scores = nt(queries, k_ref[0, n * CHUNK : (n + 1) * CHUNK, :]) * LOG_SCALE
        scores = jnp.where(limit >= n * CHUNK, scores, NEG)
        score_ref[:, n * CHUNK : (n + 1) * CHUNK] = scores
        for i in range(CHUNK // HD):
            peak = jnp.maximum(peak, scores[:, i * HD : (i + 1) * HD])
    top = jnp.max(peak, axis=1, keepdims=True).astype(BF16).astype(F32)
    base = jnp.maximum(top, FLOOR)
    acc = jnp.zeros((GROUP * DRAFTS, HD), F32)
    sums = jnp.zeros((GROUP * DRAFTS, HD), F32)
    for n in range(SLICE // CHUNK):
        weights = jnp.exp2(score_ref[:, n * CHUNK : (n + 1) * CHUNK] - base)
        for i in range(CHUNK // HD):
            sums = sums + weights[:, i * HD : (i + 1) * HD]
        acc = acc + nn(weights.astype(BF16), v_ref[0, n * CHUNK : (n + 1) * CHUNK, :])
    total = jnp.sum(sums, axis=1, keepdims=True)
    lane = lanes((GROUP * DRAFTS, HD))
    gain = gain_ref[...].astype(F32).reshape(1, 32)
    gain = jnp.broadcast_to(jnp.concatenate([gain] * 4, axis=1), (GROUP * DRAFTS, HD))
    stats = jnp.where(lane < 32, top, jnp.where(lane < 64, total, gain))
    out_ref[:, 0:16, :] = acc.astype(BF16).reshape(GROUP, DRAFTS, HD)
    out_ref[:, 16:32, :] = stats.astype(BF16).reshape(GROUP, DRAFTS, HD)


def attention(lengths, gain, queries, keys, values):
    return pl.pallas_call(
        attend,
        grid=(ROWS,),
        in_specs=[
            SMEM,
            VMEM,
            pl.BlockSpec((1, DRAFTS, GROUP * HD), lambda r: (r, 0, 0)),
            pl.BlockSpec((1, SLICE, HD), lambda r: (r, 0, 0)),
            pl.BlockSpec((1, SLICE, HD), lambda r: (r, 0, 0)),
        ],
        out_specs=pl.BlockSpec((GROUP, 32, HD), lambda r: (r, 0, 0)),
        out_shape=jax.ShapeDtypeStruct((KV, 32, HD), BF16),
        scratch_shapes=[pltpu.VMEM((GROUP * DRAFTS, SLICE), F32)],
        compiler_params=pltpu.CompilerParams(vmem_limit_bytes=56 * MIB),
        name="attention",
    )(lengths, gain, queries, keys, values)


def combine(in_ref, attn_ref, gain_ref):
    top = in_ref[:, 16:32, 0:1].astype(F32)
    total = in_ref[:, 16:32, 32:33].astype(F32)
    joint = jnp.max(top, axis=0, keepdims=True)
    factor = jnp.exp2(top - joint)
    whole = jnp.sum(total * factor, axis=0)
    acc = jnp.sum(in_ref[:, 0:16, :].astype(F32) * factor, axis=0)
    attn = (acc / whole).astype(BF16)
    attn_ref[...] = jnp.broadcast_to(attn[None], (KV, DRAFTS, HD))
    pick = lanes((KV, KV * 16)) == 16 * lax.broadcasted_iota(jnp.int32, (KV, KV * 16), 0)
    stats = in_ref[:, 16:32, :].reshape(KV * 16, HD)
    gain_ref[...] = nn(pick.astype(F32).astype(BF16), stats).astype(BF16)


def combined(parts):
    return pl.pallas_call(
        combine,
        in_specs=[VMEM],
        out_specs=[VMEM, VMEM],
        out_shape=[
            jax.ShapeDtypeStruct((KV, DRAFTS, HD), BF16),
            jax.ShapeDtypeStruct((KV, HD), BF16),
        ],
        compiler_params=pltpu.CompilerParams(vmem_limit_bytes=16 * MIB),
        name="combine",
    )(parts)


def project(attn_ref, weight_ref, residual_ref, gain_ref, own_ref, other_ref):
    core = lax.axis_index("c")
    head = lax.axis_index("x") * 2 + core
    attn = jnp.concatenate(
        [
            jnp.concatenate([attn_ref[r * GROUP + g] for g in range(GROUP)], axis=1)
            for r in range(ROWS)
        ],
        axis=0,
    )
    spread = nn(attn, weight_ref[...])
    source = lax.broadcasted_iota(jnp.int32, (32, 256), 0)
    put = (lanes((32, 256)) == head * 32 + source).astype(F32).astype(BF16)
    spread = spread + tn(residual_ref[...], put)
    source = lax.broadcasted_iota(jnp.int32, (HD, 256), 0)
    put = (lanes((HD, 256)) == head * 32 + source - 64) & (source >= 64) & (source < 96)
    gain = nn(gain_ref[...], put.astype(F32).astype(BF16))
    both = jnp.concatenate([spread, gain], axis=0)
    own_ref[...] = jnp.where(core == 0, both[:, :HD], both[:, HD:])
    other_ref[...] = jnp.where(core == 0, both[:, HD:], both[:, :HD]).astype(BF16)


def projected(attn, weight, residual, gain):
    return pl.pallas_call(
        project,
        in_specs=[VMEM] * 4,
        out_specs=[VMEM, VMEM],
        out_shape=[
            jax.ShapeDtypeStruct((TOKENS + KV, HD), F32),
            jax.ShapeDtypeStruct((TOKENS + KV, HD), BF16),
        ],
        compiler_params=pltpu.CompilerParams(vmem_limit_bytes=16 * MIB),
        name="project",
    )(attn, weight, residual, gain)


def mix(a_ref, b_ref, c_ref, d_ref, spread_ref, mixed_ref, gain_ref):
    total = (a_ref[...].astype(F32) + b_ref[...].astype(F32)) + (
        c_ref[...].astype(F32) + d_ref[...].astype(F32)
    )
    mixed = total[:TOKENS].astype(BF16)
    spread_ref[...] = jnp.broadcast_to(mixed[None], (KV, TOKENS, HD))
    mixed_ref[...] = mixed
    gain_ref[...] = total[TOKENS:]


def mixing(parts):
    return pl.pallas_call(
        mix,
        in_specs=[VMEM] * 4,
        out_specs=[VMEM, VMEM, VMEM],
        out_shape=[
            jax.ShapeDtypeStruct((KV, TOKENS, HD), BF16),
            jax.ShapeDtypeStruct((TOKENS, HD), BF16),
            jax.ShapeDtypeStruct((KV, HD), F32),
        ],
        compiler_params=pltpu.CompilerParams(vmem_limit_bytes=16 * MIB),
        name="mix",
    )(*parts)


def widen(mixed_ref, gain_ref, *refs):
    weight_refs, out_ref = refs[:4], refs[4]
    core = lax.axis_index("c")
    units = weight_refs[0].shape[0]
    squares = jnp.zeros((TOKENS, HD), F32)
    sums = jnp.zeros((TOKENS, 4 * units), F32)
    for k in range(0, KV, 2):
        scaled, weights = [], []
        for i in (k, k + 1):
            part = mixed_ref[i].astype(F32)
            squares = squares + part * part
            scaled.append((part * gain_ref[i : i + 1, :]).astype(BF16))
            at = pl.ds(pl.multiple_of(i * 256 + core * HD, HD), HD)
            weights.append(jnp.concatenate([ref[:, at] for ref in weight_refs], axis=0))
        sums = sums + nt(jnp.concatenate(scaled, axis=1), jnp.concatenate(weights, axis=1))
    square = jnp.broadcast_to(jnp.sum(squares, axis=1, keepdims=True), (TOKENS, HD - units))
    for i in range(4):
        out_ref[i] = jnp.concatenate([sums[:, i * units : (i + 1) * units], square], axis=1)


def widened(mixed, gain, weights):
    return pl.pallas_call(
        widen,
        in_specs=[VMEM] * 6,
        out_specs=VMEM,
        out_shape=jax.ShapeDtypeStruct((4, TOKENS, HD), F32),
        compiler_params=pltpu.CompilerParams(vmem_limit_bytes=16 * MIB),
        name="widen",
    )(mixed, gain, *weights)


def narrow(mine_ref, theirs_ref, own_ref, other_ref, out_ref):
    core = lax.axis_index("c")
    units = own_ref.shape[0]
    square = mine_ref[0, :, units : units + 1] + theirs_ref[0, :, units : units + 1]
    scale = lax.rsqrt(square / D + EPSILON)
    hidden = []
    for i in (0, 2):
        gate = (mine_ref[i] + theirs_ref[2 - i]) * scale
        upward = (mine_ref[i + 1] + theirs_ref[3 - i]) * scale
        hidden.append((gate / (1.0 + jnp.exp(-gate)) * upward)[:, :units])
    hidden = jnp.concatenate(hidden, axis=1).astype(BF16)
    lane = lanes((TOKENS, HD))
    for y in range(4):
        for z_high in range(2):
            tiles = [None] * 4
            for z_low in range(4):
                k = (z_high * 4 + z_low) * 4 + y
                weight = jnp.concatenate(
                    [ref[:, k * 256 : (k + 1) * 256] for ref in (own_ref, other_ref)], axis=0
                )
                terms = nn(hidden, weight)
                for x in range(4):
                    part = terms[:, x // 2 * HD : (x // 2 + 1) * HD]
                    move = (z_low - x % 2 * 2 - core + 8) % 4 * 32
                    part = pltpu.roll(part, move, 1)
                    tiles[x] = (
                        part if z_low == 0 else jnp.where(lane >= z_low * 32, part, tiles[x])
                    )
            for x in range(4):
                out_ref[y * 4 + x, z_high * TOKENS : (z_high + 1) * TOKENS, :] = tiles[x].astype(
                    BF16
                )


def narrowed(mine, theirs, own, other):
    return pl.pallas_call(
        narrow,
        in_specs=[VMEM] * 4,
        out_specs=VMEM,
        out_shape=jax.ShapeDtypeStruct((16, 2 * TOKENS, HD), BF16),
        compiler_params=pltpu.CompilerParams(vmem_limit_bytes=16 * MIB),
        name="narrow",
    )(mine, theirs, own, other)


def partial_sum(in_ref, out_ref):
    total = in_ref[0].astype(F32)
    for k in range(1, 16):
        total = total + in_ref[k].astype(F32)
    lane = lanes((16, HD))
    for z in range(8):
        packed = None
        for a in range(4):
            start = z // 4 * TOKENS + a * 16
            part = pltpu.roll(total[start : start + 16], (a - z % 4) % 4 * 32, 1)
            packed = part if a == 0 else jnp.where(lane >= a * 32, part, packed)
        out_ref[z] = packed.astype(BF16)


def summed(parts):
    return pl.pallas_call(
        partial_sum,
        in_specs=[VMEM],
        out_specs=VMEM,
        out_shape=jax.ShapeDtypeStruct((8, 16, HD), BF16),
        compiler_params=pltpu.CompilerParams(vmem_limit_bytes=16 * MIB),
        name="partial_sum",
    )(parts)


def finish(parts_ref, own_ref, other_ref, out_ref):
    x, core = lax.axis_index("x"), lax.axis_index("c")
    total = parts_ref[0].astype(F32)
    for z in range(1, 8):
        total = total + parts_ref[z].astype(F32)
    tall = jnp.concatenate([pltpu.roll(total, (4 - a) % 4 * 32, 1) for a in range(4)], axis=0)
    mixed = jnp.where(x // 2 == core, own_ref[...].astype(F32), other_ref[...].astype(F32))
    mixed = pltpu.roll(mixed, (8 - x * 2 - core) % 4 * 32, 1)
    out_ref[...] = jnp.transpose(mixed + tall)[:32].astype(BF16)


def finished(parts, own, other):
    return pl.pallas_call(
        finish,
        in_specs=[VMEM] * 3,
        out_specs=VMEM,
        out_shape=jax.ShapeDtypeStruct((32, TOKENS), BF16),
        compiler_params=pltpu.CompilerParams(vmem_limit_bytes=16 * MIB),
        name="finish",
    )(parts, own, other)


SWAP = [(0, 1), (1, 0)]


def trade(part):
    return lax.ppermute(part, "c", SWAP)


def exchange(parts, axes):
    return lax.all_to_all(parts, axes, 0, 0, tiled=True)


def shards(
    lengths,
    queries,
    cache_keys,
    cache_values,
    residual_in,
    out_weight,
    norm_gain,
    gate_weight,
    up_weight,
    down_weight,
):
    weights = [gate_weight.T, up_weight.T]
    weights = weights + [trade(weight) for weight in weights]
    other_down = trade(down_weight)
    parts = attention(lengths, norm_gain, queries, cache_keys, cache_values)
    attn, gain = combined(exchange(parts, ("z", "y")))
    attn = exchange(attn, ("z", "y"))
    own, other = projected(attn, out_weight, residual_in.T, gain)
    pair = (own + trade(other).astype(F32)).astype(BF16)
    around = [lax.ppermute(pair, "x", [(i, (i + s) % 4) for i in range(4)]) for s in (1, 2, 3)]
    spread, mixed, gain = mixing([pair] + around)
    other_mixed = trade(mixed)
    sums = widened(exchange(spread, ("z", "y")), gain, weights)
    terms = narrowed(sums, trade(sums), down_weight, other_down)
    terms = summed(exchange(terms, ("y", "x")))
    return finished(exchange(terms, "z"), mixed, other_mixed).T


def solution(mesh):
    fine = Mesh(mesh.devices.reshape(8, 4, 4, 2), ("z", "y", "x", "c"))
    kvseq, head = ("z", "y"), ("x", "c")
    every = kvseq + head
    placed = (
        P(),
        P(None, None, head),
        P(None, kvseq, head),
        P(None, kvseq, head),
        P(None, every),
        P(head, kvseq),
        P(every),
        P(None, every),
        P(None, every),
        P(every, None),
    )
    return jax.shard_map(
        shards, mesh=fine, in_specs=placed, out_specs=P(None, every), check_vma=False
    )
```

```python
import math

import jax
import jax.numpy as jnp
from jax import lax
from jax.experimental import pallas as pl
from jax.experimental.pallas import tpu as pltpu
from jax.sharding import Mesh, PartitionSpec as P

D = 8192
FF = 28672
HD = 128
GROUP = 8
ROWS = 4
DRAFTS = 16
TOKENS = 64
KV = 32
SLICE = 2048
CHUNK = 512
NEG = -1e30
FLOOR = -1e29
EPSILON = 1e-05
LOG_SCALE = math.log2(math.e) / math.sqrt(HD)
MIB = 1024 * 1024
F32 = jnp.float32
BF16 = jnp.bfloat16
VMEM = pl.BlockSpec(memory_space=pltpu.VMEM)
SMEM = pl.BlockSpec(memory_space=pltpu.SMEM)


def nt(a, b):
    return lax.dot_general(a, b, (((1,), (1,)), ((), ())), preferred_element_type=F32)


def nn(a, b):
    return jnp.dot(a, b, preferred_element_type=F32)


def tn(a, b):
    return lax.dot_general(a, b, (((0,), (0,)), ((), ())), preferred_element_type=F32)


def lanes(shape):
    return lax.broadcasted_iota(jnp.int32, shape, len(shape) - 1)


def attend(
    lengths_ref, gain_ref, q_ref, keys_ref, values_ref, out_ref, k_ref, v_ref, score_ref, sems
):
    copies = []
    for row in range(ROWS):
        copies.append(
            [
                pltpu.make_async_copy(keys_ref.at[row], k_ref.at[row], sems.at[row, 0]),
                pltpu.make_async_copy(values_ref.at[row], v_ref.at[row], sems.at[row, 1]),
            ]
        )
        for copy in copies[row]:
            copy.start()
    first_key = (lax.axis_index("z") * 4 + lax.axis_index("y")) * SLICE
    draft = lax.broadcasted_iota(jnp.int32, (GROUP * DRAFTS, CHUNK), 0) % DRAFTS
    offset = draft - DRAFTS - lanes((GROUP * DRAFTS, CHUNK)) - first_key
    gain = gain_ref[...].astype(F32).reshape(1, 32)
    gain = jnp.concatenate([gain] * 4, axis=1).reshape(1, 1, HD)
    lane = lanes((GROUP, 8, HD))
    for row in range(ROWS):
        queries = jnp.concatenate(
            [q_ref[row, :, g * HD : (g + 1) * HD] for g in range(GROUP)], axis=0
        )
        limit = offset + lengths_ref[row]
        peak = jnp.full((GROUP * DRAFTS, HD), NEG, F32)
        copies[row][0].wait()
        for n in range(SLICE // CHUNK):
            scores = nt(queries, k_ref[row, n * CHUNK : (n + 1) * CHUNK, :]) * LOG_SCALE
            scores = jnp.where(limit >= n * CHUNK, scores, NEG)
            score_ref[row % 2, :, n * CHUNK : (n + 1) * CHUNK] = scores
            for i in range(CHUNK // HD):
                peak = jnp.maximum(peak, scores[:, i * HD : (i + 1) * HD])
        top = jnp.max(peak, axis=1, keepdims=True).astype(BF16).astype(F32)
        base = jnp.maximum(top, FLOOR)
        acc = jnp.zeros((GROUP * DRAFTS, HD), F32)
        sums = jnp.zeros((GROUP * DRAFTS, HD), F32)
        copies[row][1].wait()
        for n in range(SLICE // CHUNK):
            weights = jnp.exp2(score_ref[row % 2, :, n * CHUNK : (n + 1) * CHUNK] - base)
            for i in range(CHUNK // HD):
                sums = sums + weights[:, i * HD : (i + 1) * HD]
            acc = acc + nn(weights.astype(BF16), v_ref[row, n * CHUNK : (n + 1) * CHUNK, :])
        total = jnp.sum(sums, axis=1, keepdims=True).reshape(GROUP, DRAFTS, 1)
        top = top.reshape(GROUP, DRAFTS, 1)
        stats = jnp.where(lane < 64, total[:, 8:], gain)
        stats = jnp.where(lane < 48, total[:, :8], stats)
        stats = jnp.where(lane < 32, top[:, 8:], stats)
        stats = jnp.where(lane < 16, top[:, :8], stats)
        acc = acc.reshape(GROUP, DRAFTS, HD)
        block = jnp.concatenate([acc, stats], axis=1).astype(BF16)
        out_ref[row * GROUP : (row + 1) * GROUP] = block


def attention(lengths, gain, queries, keys, values):
    held = pl.BlockSpec(memory_space=pltpu.HBM)
    return pl.pallas_call(
        attend,
        in_specs=[SMEM, VMEM, VMEM, held, held],
        out_specs=VMEM,
        out_shape=jax.ShapeDtypeStruct((KV, 24, HD), BF16),
        scratch_shapes=[
            pltpu.VMEM((ROWS, SLICE, HD), BF16),
            pltpu.VMEM((ROWS, SLICE, HD), BF16),
            pltpu.VMEM((2, GROUP * DRAFTS, SLICE), F32),
            pltpu.SemaphoreType.DMA((ROWS, 2)),
        ],
        compiler_params=pltpu.CompilerParams(vmem_limit_bytes=57 * MIB),
        cost_estimate=pl.CostEstimate(
            flops=0, bytes_accessed=12800000, transcendentals=0
        ),
        name="attention",
    )(lengths, gain, queries, keys, values)


def combine(in_ref, attn_ref, gain_ref):
    parts = in_ref[...].astype(F32)
    stats = parts[:, 16:24]
    top = jnp.concatenate([stats[:, :, 0:1], stats[:, :, 16:17]], axis=1)
    total = jnp.concatenate([stats[:, :, 32:33], stats[:, :, 48:49]], axis=1)
    joint = jnp.max(top, axis=0, keepdims=True)
    factor = jnp.exp2(top - joint)
    whole = jnp.sum(total * factor, axis=0)
    acc = jnp.sum(parts[:, 0:16] * factor, axis=0)
    attn = (acc / whole).astype(BF16)
    attn_ref[...] = jnp.broadcast_to(attn[None], (KV, DRAFTS, HD))
    pick = lanes((KV, KV * 8)) == 8 * lax.broadcasted_iota(jnp.int32, (KV, KV * 8), 0)
    stats = stats.reshape(KV * 8, HD).astype(BF16)
    gain_ref[...] = nn(pick.astype(F32).astype(BF16), stats).astype(BF16)


def combined(parts):
    return pl.pallas_call(
        combine,
        in_specs=[VMEM],
        out_specs=[VMEM, VMEM],
        out_shape=[
            jax.ShapeDtypeStruct((KV, DRAFTS, HD), BF16),
            jax.ShapeDtypeStruct((KV, HD), BF16),
        ],
        compiler_params=pltpu.CompilerParams(vmem_limit_bytes=16 * MIB),
        cost_estimate=pl.CostEstimate(
            flops=0, bytes_accessed=38400000, transcendentals=0
        ),
        name="combine",
    )(parts)


def project(attn_ref, weight_ref, residual_ref, gain_ref, out_ref):
    head = lax.axis_index("x") * 2 + lax.axis_index("c")
    attn = jnp.concatenate(
        [
            jnp.concatenate([attn_ref[r * GROUP + g] for g in range(GROUP)], axis=1)
            for r in range(ROWS)
        ],
        axis=0,
    )
    spread = nn(attn, weight_ref[...])
    source = lax.broadcasted_iota(jnp.int32, (32, 256), 0)
    put = (lanes((32, 256)) == head * 32 + source).astype(F32).astype(BF16)
    spread = spread + tn(residual_ref[...], put)
    source = lax.broadcasted_iota(jnp.int32, (HD, 256), 0)
    put = (lanes((HD, 256)) == head * 32 + source - 64) & (source >= 64) & (source < 96)
    gain = nn(gain_ref[...], put.astype(F32).astype(BF16))
    both = jnp.concatenate([spread, gain], axis=0).astype(BF16)
    for i in range(8):
        out_ref[i, : TOKENS + KV] = both[:, i % 2 * HD : (i % 2 + 1) * HD]
    spot = lanes((DRAFTS, HD)) // 32
    for half in range(2):
        part = spread[:, half * HD : (half + 1) * HD]
        rows = [part[a * DRAFTS : (a + 1) * DRAFTS] for a in range(4)]
        rows = [pltpu.roll(row, a * 32, 1) if a else row for a, row in enumerate(rows)]
        for i in range(4):
            tile = rows[0]
            for a in range(1, 4):
                tile = jnp.where(spot == (i + a) % 4, rows[a], tile)
            out_ref[half * 4 + i, TOKENS + KV :] = tile.astype(BF16)


def projected(attn, weight, residual, gain):
    return pl.pallas_call(
        project,
        in_specs=[VMEM] * 4,
        out_specs=VMEM,
        out_shape=jax.ShapeDtypeStruct((8, TOKENS + KV + DRAFTS, HD), BF16),
        compiler_params=pltpu.CompilerParams(vmem_limit_bytes=8 * MIB),
        cost_estimate=pl.CostEstimate(
            flops=0, bytes_accessed=3200000, transcendentals=0
        ),
        name="project",
    )(attn, weight, residual, gain)


def mix(in_ref, *refs):
    spread_ref, mixed_ref, gain_ref = refs[-3:]
    total = in_ref[0].astype(F32)
    for i in range(1, 8):
        total = total + in_ref[i].astype(F32)
    spread_ref[...] = jnp.broadcast_to(total[:TOKENS].astype(BF16)[None], (KV, TOKENS, HD))
    gain_ref[...] = total[TOKENS : TOKENS + KV]
    mixed_ref[...] = total[TOKENS + KV :].astype(BF16)


def mixing(parts, held):
    return pl.pallas_call(
        mix,
        in_specs=[VMEM] + [pl.BlockSpec(memory_space=pl.ANY)] * len(held),
        out_specs=[VMEM, VMEM, VMEM],
        out_shape=[
            jax.ShapeDtypeStruct((KV, TOKENS, HD), BF16),
            jax.ShapeDtypeStruct((DRAFTS, HD), BF16),
            jax.ShapeDtypeStruct((KV, HD), F32),
        ],
        compiler_params=pltpu.CompilerParams(vmem_limit_bytes=8 * MIB),
        cost_estimate=pl.CostEstimate(
            flops=0, bytes_accessed=38400000, transcendentals=0
        ),
        name="mix",
    )(parts, *held)


def widen(mixed_ref, gain_ref, *refs):
    weight_refs, out_ref = refs[:4], refs[4]
    core = lax.axis_index("c")
    units = weight_refs[0].shape[0]
    squares = jnp.zeros((TOKENS, HD), F32)
    sums = [jnp.zeros((units, TOKENS), F32) for _ in weight_refs]
    for k in range(0, KV, 2):
        scaled, places = [], []
        for i in (k, k + 1):
            part = mixed_ref[i].astype(F32)
            squares = squares + part * part
            scaled.append((part * gain_ref[i : i + 1, :]).astype(BF16))
            places.append(pl.ds(pl.multiple_of(i * 256 + core * HD, HD), HD))
        scaled = jnp.concatenate(scaled, axis=1)
        for i, ref in enumerate(weight_refs):
            weight = jnp.concatenate([ref[:, at] for at in places], axis=1)
            sums[i] = sums[i] + nt(weight, scaled)
    square = jnp.sum(jnp.transpose(squares), axis=0, keepdims=True)
    square = jnp.broadcast_to(square, (8, TOKENS))
    own = jnp.concatenate([sums[0], sums[1], square], axis=0)
    other = jnp.concatenate([sums[2], sums[3], square], axis=0)
    out_ref[...] = jnp.concatenate([own, other], axis=1)


def widened(mixed, gain, weights):
    return pl.pallas_call(
        widen,
        in_specs=[VMEM] * 6,
        out_specs=VMEM,
        out_shape=jax.ShapeDtypeStruct((2 * weights[0].shape[0] + 8, HD), F32),
        compiler_params=pltpu.CompilerParams(vmem_limit_bytes=16 * MIB),
        cost_estimate=pl.CostEstimate(
            flops=0, bytes_accessed=6400000, transcendentals=0
        ),
        name="widen",
    )(mixed, gain, *weights)


def narrow(mine_ref, theirs_ref, own_ref, other_ref, out_ref):
    core = lax.axis_index("c")
    units = own_ref.shape[0]
    total = mine_ref[...] + pltpu.roll(theirs_ref[...], TOKENS, 1)
    scale = lax.rsqrt(total[2 * units : 2 * units + 1] / D + EPSILON)
    gate = total[:units] * scale
    upward = total[units : 2 * units] * scale
    hidden = jnp.transpose(gate / (1.0 + jnp.exp(-gate)) * upward)
    hidden = jnp.concatenate([hidden[:TOKENS], hidden[TOKENS:]], axis=1).astype(BF16)
    spot = lanes((TOKENS, HD)) // 32
    masks = [spot == (core + i) % 4 for i in range(4)]
    for y in range(4):
        for z_high in range(2):
            tiles = [None] * 4
            for z_low in range(4):
                k = (z_high * 4 + z_low) * 4 + y
                weight = jnp.concatenate(
                    [ref[:, k * 256 : (k + 1) * 256] for ref in (own_ref, other_ref)], axis=0
                )
                terms = nn(hidden, weight)
                for half in range(2):
                    part = terms[:, half * HD : (half + 1) * HD]
                    if z_low:
                        part = pltpu.roll(part, z_low * 32, 1)
                    for odd in range(2):
                        x = 2 * half + odd
                        mask = masks[(2 * odd + z_low) % 4]
                        tiles[x] = jnp.where(mask, part, tiles[x]) if z_low else part
            for x in range(4):
                out_ref[y * 4 + x, z_high * TOKENS : (z_high + 1) * TOKENS, :] = tiles[x].astype(
                    BF16
                )


def narrowed(mine, theirs, own, other):
    return pl.pallas_call(
        narrow,
        in_specs=[VMEM] * 4,
        out_specs=VMEM,
        out_shape=jax.ShapeDtypeStruct((16, 2 * TOKENS, HD), BF16),
        compiler_params=pltpu.CompilerParams(vmem_limit_bytes=16 * MIB),
        cost_estimate=pl.CostEstimate(
            flops=0, bytes_accessed=6400000, transcendentals=0
        ),
        name="narrow",
    )(mine, theirs, own, other)


def partial_sum(in_ref, out_ref):
    total = in_ref[0].astype(F32)
    for k in range(1, 16):
        total = total + in_ref[k].astype(F32)
    shift = lax.axis_index("x") * 2 + lax.axis_index("c")
    total = pltpu.roll(total, (8 - shift) % 4 * 32, 1)
    lane = lanes((16, HD))
    for z in range(8):
        packed = None
        for a in range(4):
            start = z // 4 * TOKENS + a * 16
            part = pltpu.roll(total[start : start + 16], (a - z % 4) % 4 * 32, 1)
            packed = part if a == 0 else jnp.where(lane >= a * 32, part, packed)
        out_ref[z] = packed.astype(BF16)


def summed(parts):
    return pl.pallas_call(
        partial_sum,
        in_specs=[VMEM],
        out_specs=VMEM,
        out_shape=jax.ShapeDtypeStruct((8, 16, HD), BF16),
        compiler_params=pltpu.CompilerParams(vmem_limit_bytes=16 * MIB),
        cost_estimate=pl.CostEstimate(
            flops=0, bytes_accessed=3200000, transcendentals=0
        ),
        name="partial_sum",
    )(parts)


def finish(parts_ref, mixed_ref, out_ref):
    total = parts_ref[0].astype(F32)
    for z in range(1, 8):
        total = total + parts_ref[z].astype(F32)
    shift = lax.axis_index("x") * 2 + lax.axis_index("c")
    total = total + pltpu.roll(mixed_ref[...].astype(F32), (8 - shift) % 4 * 32, 1)
    tall = jnp.concatenate([pltpu.roll(total, (4 - a) % 4 * 32, 1) for a in range(4)], axis=0)
    out_ref[...] = jnp.transpose(tall)[:32].astype(BF16)


def finished(parts, mixed):
    return pl.pallas_call(
        finish,
        in_specs=[VMEM] * 2,
        out_specs=VMEM,
        out_shape=jax.ShapeDtypeStruct((32, TOKENS), BF16),
        compiler_params=pltpu.CompilerParams(vmem_limit_bytes=8 * MIB),
        cost_estimate=pl.CostEstimate(
            flops=0, bytes_accessed=3200000, transcendentals=0
        ),
        name="finish",
    )(parts, mixed)


SWAP = [(0, 1), (1, 0)]


def trade(part):
    return lax.ppermute(part, "c", SWAP)


def exchange(parts, axes):
    return lax.all_to_all(parts, axes, 0, 0, tiled=True)


def shards(
    lengths,
    queries,
    cache_keys,
    cache_values,
    residual_in,
    out_weight,
    norm_gain,
    gate_weight,
    up_weight,
    down_weight,
):
    weights = [gate_weight.T, up_weight.T]
    parts = attention(lengths, norm_gain, queries, cache_keys, cache_values)
    parts, weights, down_weight = lax.optimization_barrier((parts, weights, down_weight))
    weights = weights + [trade(weight) for weight in weights]
    other_down = trade(down_weight)
    attn, gain = combined(exchange(parts, ("z", "y")))
    attn = exchange(attn, ("z", "y"))
    parts = exchange(projected(attn, out_weight, residual_in.T, gain), ("x", "c"))
    spread, mixed, gain = mixing(parts, weights + [down_weight, other_down])
    sums = widened(exchange(spread, ("z", "y")), gain, weights)
    terms = narrowed(sums, trade(sums), down_weight, other_down)
    terms = summed(exchange(terms, ("y", "x")))
    return finished(exchange(terms, "z"), mixed).T


def solution(mesh):
    fine = Mesh(mesh.devices.reshape(8, 4, 4, 2), ("z", "y", "x", "c"))
    kvseq, head = ("z", "y"), ("x", "c")
    every = kvseq + head
    placed = (
        P(),
        P(None, None, head),
        P(None, kvseq, head),
        P(None, kvseq, head),
        P(None, every),
        P(head, kvseq),
        P(every),
        P(None, every),
        P(None, every),
        P(every, None),
    )
    return jax.shard_map(
        shards, mesh=fine, in_specs=placed, out_specs=P(None, every), check_vma=False
    )
```

```python
import math

import jax
import jax.numpy as jnp
from jax import lax
from jax.experimental import pallas as pl
from jax.experimental.pallas import tpu as pltpu
from jax.sharding import Mesh, PartitionSpec as P

D = 8192
FF = 28672
HD = 128
GROUP = 8
ROWS = 4
DRAFTS = 16
TOKENS = 64
KV = 32
SLICE = 2048
CHUNK = 512
NEG = -1e30
FLOOR = -1e29
EPSILON = 1e-05
LOG_SCALE = math.log2(math.e) / math.sqrt(HD)
MIB = 1024 * 1024
F32 = jnp.float32
BF16 = jnp.bfloat16
VMEM = pl.BlockSpec(memory_space=pltpu.VMEM)
SMEM = pl.BlockSpec(memory_space=pltpu.SMEM)


def nt(a, b):
    return lax.dot_general(a, b, (((1,), (1,)), ((), ())), preferred_element_type=F32)


def nn(a, b):
    return jnp.dot(a, b, preferred_element_type=F32)


def tn(a, b):
    return lax.dot_general(a, b, (((0,), (0,)), ((), ())), preferred_element_type=F32)


def lanes(shape):
    return lax.broadcasted_iota(jnp.int32, shape, len(shape) - 1)


def attend(
    lengths_ref, gain_ref, queries_ref, keys_ref, values_ref, out_ref,
    q_ref, k_ref, v_ref, score_ref, sems,
):
    copies = []
    pairs = [(queries_ref, q_ref), (keys_ref, k_ref), (values_ref, v_ref)]
    for n, (first, last) in enumerate([(0, 1), (1, ROWS)]):
        copies.append(
            [
                pltpu.make_async_copy(a.at[first:last], b.at[first:last], sems.at[n, i])
                for i, (a, b) in enumerate(pairs)
            ]
        )
        for i in (1, 0, 2):
            copies[n][i].start()
    first_key = (lax.axis_index("z") * 4 + lax.axis_index("y")) * SLICE
    draft = lax.broadcasted_iota(jnp.int32, (GROUP * DRAFTS, CHUNK), 0) % DRAFTS
    offset = draft - DRAFTS - lanes((GROUP * DRAFTS, CHUNK)) - first_key
    gain = gain_ref[...].astype(F32).reshape(1, 32)
    gain = jnp.concatenate([gain] * 4, axis=1).reshape(1, 1, HD)
    lane = lanes((GROUP, 8, HD))
    for row in range(ROWS):
        if row < 2:
            copies[row][0].wait()
        queries = jnp.concatenate(
            [q_ref[row, :, g * HD : (g + 1) * HD] for g in range(GROUP)], axis=0
        )
        limit = offset + lengths_ref[row]
        peak = jnp.full((GROUP * DRAFTS, HD), NEG, F32)
        if row < 2:
            copies[row][1].wait()
        for n in range(SLICE // CHUNK):
            scores = nt(queries, k_ref[row, n * CHUNK : (n + 1) * CHUNK, :]) * LOG_SCALE
            scores = jnp.where(limit >= n * CHUNK, scores, NEG)
            score_ref[row % 2, :, n * CHUNK : (n + 1) * CHUNK] = scores
            for i in range(CHUNK // HD):
                peak = jnp.maximum(peak, scores[:, i * HD : (i + 1) * HD])
        top = jnp.max(peak, axis=1, keepdims=True).astype(BF16).astype(F32)
        base = jnp.maximum(top, FLOOR)
        acc = jnp.zeros((GROUP * DRAFTS, HD), F32)
        sums = jnp.zeros((GROUP * DRAFTS, HD), F32)
        if row < 2:
            copies[row][2].wait()
        for n in range(SLICE // CHUNK):
            weights = jnp.exp2(score_ref[row % 2, :, n * CHUNK : (n + 1) * CHUNK] - base)
            for i in range(CHUNK // HD):
                sums = sums + weights[:, i * HD : (i + 1) * HD]
            acc = acc + nn(weights.astype(BF16), v_ref[row, n * CHUNK : (n + 1) * CHUNK, :])
        total = jnp.sum(sums, axis=1, keepdims=True).reshape(GROUP, DRAFTS, 1)
        top = top.reshape(GROUP, DRAFTS, 1)
        stats = jnp.where(lane < 64, total[:, 8:], gain)
        stats = jnp.where(lane < 48, total[:, :8], stats)
        stats = jnp.where(lane < 32, top[:, 8:], stats)
        stats = jnp.where(lane < 16, top[:, :8], stats)
        acc = acc.reshape(GROUP, DRAFTS, HD)
        block = jnp.concatenate([acc, stats], axis=1).astype(BF16)
        out_ref[row * GROUP : (row + 1) * GROUP] = block


def attention(lengths, gain, queries, keys, values):
    held = pl.BlockSpec(memory_space=pltpu.HBM)
    return pl.pallas_call(
        attend,
        in_specs=[SMEM, VMEM, held, held, held],
        out_specs=VMEM,
        out_shape=jax.ShapeDtypeStruct((KV, 24, HD), BF16),
        scratch_shapes=[
            pltpu.VMEM((ROWS, DRAFTS, GROUP * HD), BF16),
            pltpu.VMEM((ROWS, SLICE, HD), BF16),
            pltpu.VMEM((ROWS, SLICE, HD), BF16),
            pltpu.VMEM((2, GROUP * DRAFTS, SLICE), F32),
            pltpu.SemaphoreType.DMA((2, 3)),
        ],
        compiler_params=pltpu.CompilerParams(vmem_limit_bytes=57 * MIB),
        name="attention",
    )(lengths, gain, queries, keys, values)


def combine(in_ref, attn_ref, gain_ref):
    parts = in_ref[...].astype(F32)
    stats = parts[:, 16:24]
    top = jnp.concatenate([stats[:, :, 0:1], stats[:, :, 16:17]], axis=1)
    total = jnp.concatenate([stats[:, :, 32:33], stats[:, :, 48:49]], axis=1)
    joint = jnp.max(top, axis=0, keepdims=True)
    factor = jnp.exp2(top - joint)
    whole = jnp.sum(total * factor, axis=0)
    acc = jnp.sum(parts[:, 0:16] * factor, axis=0)
    attn = (acc / whole).astype(BF16)
    attn_ref[...] = jnp.broadcast_to(attn[None], (KV, DRAFTS, HD))
    pick = lanes((KV, KV * 8)) == 8 * lax.broadcasted_iota(jnp.int32, (KV, KV * 8), 0)
    stats = stats.reshape(KV * 8, HD).astype(BF16)
    gain_ref[...] = nn(pick.astype(F32).astype(BF16), stats).astype(BF16)


def combined(parts):
    return pl.pallas_call(
        combine,
        in_specs=[VMEM],
        out_specs=[VMEM, VMEM],
        out_shape=[
            jax.ShapeDtypeStruct((KV, DRAFTS, HD), BF16),
            jax.ShapeDtypeStruct((KV, HD), BF16),
        ],
        compiler_params=pltpu.CompilerParams(vmem_limit_bytes=16 * MIB),
        cost_estimate=pl.CostEstimate(
            flops=10000000000, bytes_accessed=0, transcendentals=0
        ),
        name="combine",
    )(parts)


def project(attn_ref, weight_ref, residual_ref, gain_ref, *refs):
    own_ref, other_ref = refs[-2:]
    head = lax.axis_index("x") * 2 + lax.axis_index("c")
    attn = jnp.concatenate(
        [
            jnp.concatenate([attn_ref[r * GROUP + g] for g in range(GROUP)], axis=1)
            for r in range(ROWS)
        ],
        axis=0,
    )
    spread = nn(attn, weight_ref[...])
    source = lax.broadcasted_iota(jnp.int32, (32, 256), 0)
    put = (lanes((32, 256)) == head * 32 + source).astype(F32).astype(BF16)
    spread = spread + tn(residual_ref[...], put)
    source = lax.broadcasted_iota(jnp.int32, (HD, 256), 0)
    put = (lanes((HD, 256)) == head * 32 + source - 64) & (source >= 64) & (source < 96)
    gain = nn(gain_ref[...], put.astype(F32).astype(BF16))
    both = jnp.concatenate([spread, gain], axis=0)
    core = lax.axis_index("c")
    own_ref[: TOKENS + KV] = jnp.where(core == 0, both[:, :HD], both[:, HD:])
    other_ref[: TOKENS + KV] = jnp.where(core == 0, both[:, HD:], both[:, :HD]).astype(BF16)
    spot = lanes((DRAFTS, HD)) // 32
    for half in range(2):
        part = spread[:, half * HD : (half + 1) * HD]
        rows = [part[a * DRAFTS : (a + 1) * DRAFTS] for a in range(4)]
        rows = [pltpu.roll(row, a * 32, 1) if a else row for a, row in enumerate(rows)]
        for i in range(0, 4, 2):
            tiles = []
            for j in (i, i + 1):
                tile = rows[0]
                for a in range(1, 4):
                    tile = jnp.where(spot == (j + a) % 4, rows[a], tile)
                tiles.append(tile)
            start = TOKENS + KV + (half * 2 + i // 2) * DRAFTS
            own_ref[start : start + DRAFTS] = jnp.where(core == 0, tiles[0], tiles[1])
            other_ref[start : start + DRAFTS] = jnp.where(core == 0, tiles[1], tiles[0]).astype(BF16)


def projected(attn, weight, residual, gain, held):
    return pl.pallas_call(
        project,
        in_specs=[VMEM] * 4 + [pl.BlockSpec(memory_space=pl.ANY)] * len(held),
        out_specs=[VMEM, VMEM],
        out_shape=[
            jax.ShapeDtypeStruct((TOKENS + KV + 4 * DRAFTS, HD), F32),
            jax.ShapeDtypeStruct((TOKENS + KV + 4 * DRAFTS, HD), BF16),
        ],
        compiler_params=pltpu.CompilerParams(vmem_limit_bytes=8 * MIB),
        cost_estimate=pl.CostEstimate(
            flops=1000000000, bytes_accessed=0, transcendentals=0
        ),
        name="project",
    )(attn, weight, residual, gain, *held)


def pair(own_ref, other_ref, *refs):
    sum_ref = refs[4]
    sum_ref[...] = own_ref[...] + other_ref[...].astype(F32)
    common = sum_ref[: TOKENS + KV].astype(BF16)
    for s in range(4):
        x = (lax.axis_index("x") + s) % 4
        start = pl.multiple_of(TOKENS + KV + x * DRAFTS, DRAFTS)
        refs[s][: TOKENS + KV] = common
        refs[s][TOKENS + KV :] = sum_ref[pl.ds(start, DRAFTS), :].astype(BF16)


def paired(own, other):
    shape = jax.ShapeDtypeStruct((TOKENS + KV + DRAFTS, HD), BF16)
    return pl.pallas_call(
        pair,
        in_specs=[VMEM, VMEM],
        out_specs=[VMEM] * 4,
        out_shape=[shape] * 4,
        scratch_shapes=[pltpu.VMEM((TOKENS + KV + 4 * DRAFTS, HD), F32)],
        compiler_params=pltpu.CompilerParams(vmem_limit_bytes=8 * MIB),
        name="pair",
    )(own, other)


def mix(*refs):
    parts = refs[:4]
    spread_ref, mixed_ref, gain_ref = refs[-3:]
    total = (parts[0][...].astype(F32) + parts[1][...].astype(F32)) + (
        parts[2][...].astype(F32) + parts[3][...].astype(F32)
    )
    spread_ref[...] = jnp.broadcast_to(total[:TOKENS].astype(BF16)[None], (KV, TOKENS, HD))
    gain_ref[...] = total[TOKENS : TOKENS + KV]
    mixed_ref[...] = total[TOKENS + KV :].astype(BF16)


def mixing(parts, held):
    return pl.pallas_call(
        mix,
        in_specs=[VMEM] * 4 + [pl.BlockSpec(memory_space=pl.ANY)] * len(held),
        out_specs=[VMEM, VMEM, VMEM],
        out_shape=[
            jax.ShapeDtypeStruct((KV, TOKENS, HD), BF16),
            jax.ShapeDtypeStruct((DRAFTS, HD), BF16),
            jax.ShapeDtypeStruct((KV, HD), F32),
        ],
        compiler_params=pltpu.CompilerParams(vmem_limit_bytes=8 * MIB),
        cost_estimate=pl.CostEstimate(
            flops=1000000000, bytes_accessed=0, transcendentals=0
        ),
        name="mix",
    )(*parts, *held)


def widen(mixed_ref, gain_ref, *refs):
    weight_refs, out_ref = refs[:4], refs[4]
    core = lax.axis_index("c")
    units = weight_refs[0].shape[0]
    squares = jnp.zeros((TOKENS, HD), F32)
    sums = [jnp.zeros((units, TOKENS), F32) for _ in weight_refs]
    for k in range(0, KV, 2):
        scaled, places = [], []
        for i in (k, k + 1):
            part = mixed_ref[i].astype(F32)
            squares = squares + part * part
            scaled.append((part * gain_ref[i : i + 1, :]).astype(BF16))
            places.append(pl.ds(pl.multiple_of(i * 256 + core * HD, HD), HD))
        scaled = jnp.concatenate(scaled, axis=1)
        for i, ref in enumerate(weight_refs):
            weight = jnp.concatenate([ref[:, at] for at in places], axis=1)
            sums[i] = sums[i] + nt(weight, scaled)
    square = jnp.sum(jnp.transpose(squares), axis=0, keepdims=True)
    square = jnp.broadcast_to(square, (8, TOKENS))
    own = jnp.concatenate([sums[0], sums[1], square], axis=0)
    other = jnp.concatenate([sums[2], sums[3], square], axis=0)
    out_ref[...] = jnp.concatenate([own, other], axis=1)


def widened(mixed, gain, weights):
    return pl.pallas_call(
        widen,
        in_specs=[VMEM] * 6,
        out_specs=VMEM,
        out_shape=jax.ShapeDtypeStruct((2 * weights[0].shape[0] + 8, HD), F32),
        compiler_params=pltpu.CompilerParams(vmem_limit_bytes=16 * MIB),
        name="widen",
    )(mixed, gain, *weights)


def narrow(mine_ref, theirs_ref, own_ref, other_ref, out_ref):
    core = lax.axis_index("c")
    units = own_ref.shape[0]
    total = mine_ref[...] + pltpu.roll(theirs_ref[...], TOKENS, 1)
    scale = lax.rsqrt(total[2 * units : 2 * units + 1] / D + EPSILON)
    gate = total[:units] * scale
    upward = total[units : 2 * units] * scale
    hidden = jnp.transpose(gate / (1.0 + jnp.exp(-gate)) * upward)
    hidden = jnp.concatenate([hidden[:TOKENS], hidden[TOKENS:]], axis=1).astype(BF16)
    spot = lanes((TOKENS, HD)) // 32
    masks = [spot == (core + i) % 4 for i in range(4)]
    for y in range(4):
        for z_high in range(2):
            tiles = [None] * 4
            for z_low in range(4):
                k = (z_high * 4 + z_low) * 4 + y
                weight = jnp.concatenate(
                    [ref[:, k * 256 : (k + 1) * 256] for ref in (own_ref, other_ref)], axis=0
                )
                terms = nn(hidden, weight)
                for half in range(2):
                    part = terms[:, half * HD : (half + 1) * HD]
                    if z_low:
                        part = pltpu.roll(part, z_low * 32, 1)
                    for odd in range(2):
                        x = 2 * half + odd
                        mask = masks[(2 * odd + z_low) % 4]
                        tiles[x] = jnp.where(mask, part, tiles[x]) if z_low else part
            for x in range(4):
                out_ref[y * 4 + x, z_high * TOKENS : (z_high + 1) * TOKENS, :] = tiles[x].astype(
                    BF16
                )


def narrowed(mine, theirs, own, other):
    return pl.pallas_call(
        narrow,
        in_specs=[VMEM] * 4,
        out_specs=VMEM,
        out_shape=jax.ShapeDtypeStruct((16, 2 * TOKENS, HD), BF16),
        compiler_params=pltpu.CompilerParams(vmem_limit_bytes=16 * MIB),
        name="narrow",
    )(mine, theirs, own, other)


def partial_sum(in_ref, out_ref):
    total = in_ref[0].astype(F32)
    for k in range(1, 16):
        total = total + in_ref[k].astype(F32)
    shift = lax.axis_index("x") * 2 + lax.axis_index("c")
    total = pltpu.roll(total, (8 - shift) % 4 * 32, 1)
    lane = lanes((16, HD))
    for z in range(8):
        packed = None
        for a in range(4):
            start = z // 4 * TOKENS + a * 16
            part = pltpu.roll(total[start : start + 16], (a - z % 4) % 4 * 32, 1)
            packed = part if a == 0 else jnp.where(lane >= a * 32, part, packed)
        out_ref[z] = packed.astype(BF16)


def summed(parts):
    return pl.pallas_call(
        partial_sum,
        in_specs=[VMEM],
        out_specs=VMEM,
        out_shape=jax.ShapeDtypeStruct((8, 16, HD), BF16),
        compiler_params=pltpu.CompilerParams(vmem_limit_bytes=16 * MIB),
        name="partial_sum",
    )(parts)


def finish(parts_ref, mixed_ref, out_ref):
    total = parts_ref[0].astype(F32)
    for z in range(1, 8):
        total = total + parts_ref[z].astype(F32)
    shift = lax.axis_index("x") * 2 + lax.axis_index("c")
    total = total + pltpu.roll(mixed_ref[...].astype(F32), (8 - shift) % 4 * 32, 1)
    tall = jnp.concatenate([pltpu.roll(total, (4 - a) % 4 * 32, 1) for a in range(4)], axis=0)
    out_ref[...] = jnp.transpose(tall)[:32].astype(BF16)


def finished(parts, mixed):
    return pl.pallas_call(
        finish,
        in_specs=[VMEM] * 2,
        out_specs=VMEM,
        out_shape=jax.ShapeDtypeStruct((32, TOKENS), BF16),
        compiler_params=pltpu.CompilerParams(vmem_limit_bytes=8 * MIB),
        name="finish",
    )(parts, mixed)


SWAP = [(0, 1), (1, 0)]


def trade(part):
    return lax.ppermute(part, "c", SWAP)


def exchange(parts, axes):
    return lax.all_to_all(parts, axes, 0, 0, tiled=True)


def shards(
    lengths,
    queries,
    cache_keys,
    cache_values,
    residual_in,
    out_weight,
    norm_gain,
    gate_weight,
    up_weight,
    down_weight,
):
    weights = [gate_weight.T, up_weight.T]
    parts = attention(lengths, norm_gain, queries, cache_keys, cache_values)
    parts, weights, down_weight = lax.optimization_barrier((parts, weights, down_weight))
    weights = weights + [trade(weight) for weight in weights]
    other_down = trade(down_weight)
    attn, gain = combined(exchange(parts, ("z", "y")))
    attn = exchange(attn, ("z", "y"))
    own, other = projected(attn, out_weight, residual_in.T, gain, weights[2:] + [other_down])
    parts = list(paired(own, trade(other)))
    parts[1:] = [
        lax.ppermute(part, "x", [(i, (i + s) % 4) for i in range(4)])
        for s, part in enumerate(parts[1:], 1)
    ]
    spread, mixed, gain = mixing(parts, [])
    sums = widened(exchange(spread, ("z", "y")), gain, weights)
    terms = narrowed(sums, trade(sums), down_weight, other_down)
    terms = summed(exchange(terms, ("y", "x")))
    return finished(exchange(terms, "z"), mixed).T


def solution(mesh):
    fine = Mesh(mesh.devices.reshape(8, 4, 4, 2), ("z", "y", "x", "c"))
    kvseq, head = ("z", "y"), ("x", "c")
    every = kvseq + head
    placed = (
        P(),
        P(None, None, head),
        P(None, kvseq, head),
        P(None, kvseq, head),
        P(None, every),
        P(head, kvseq),
        P(every),
        P(None, every),
        P(None, every),
        P(every, None),
    )
    return jax.shard_map(
        shards, mesh=fine, in_specs=placed, out_specs=P(None, every), check_vma=False
    )
```

```python
import math

import jax
import jax.numpy as jnp
from jax import lax
from jax.experimental import pallas as pl
from jax.experimental.pallas import tpu as pltpu
from jax.sharding import Mesh, PartitionSpec as P

D = 8192
FF = 28672
HD = 128
GROUP = 8
ROWS = 4
DRAFTS = 16
TOKENS = 64
KV = 32
SLICE = 2048
CHUNK = 512
NEG = -1e30
FLOOR = -1e29
EPSILON = 1e-05
LOG_SCALE = math.log2(math.e) / math.sqrt(HD)
MIB = 1024 * 1024
F32 = jnp.float32
BF16 = jnp.bfloat16
VMEM = pl.BlockSpec(memory_space=pltpu.VMEM)
SMEM = pl.BlockSpec(memory_space=pltpu.SMEM)


def nt(a, b):
    return lax.dot_general(a, b, (((1,), (1,)), ((), ())), preferred_element_type=F32)


def nn(a, b):
    return jnp.dot(a, b, preferred_element_type=F32)


def tn(a, b):
    return lax.dot_general(a, b, (((0,), (0,)), ((), ())), preferred_element_type=F32)


def lanes(shape):
    return lax.broadcasted_iota(jnp.int32, shape, len(shape) - 1)


def attend(
    lengths_ref, gain_ref, queries_ref, keys_ref, values_ref, out_ref,
    q_ref, k_ref, v_ref, score_ref, sems,
):
    copies = []
    pairs = [(queries_ref, q_ref), (keys_ref, k_ref), (values_ref, v_ref)]
    for n, (first, last) in enumerate([(0, 1), (1, ROWS)]):
        copies.append(
            [
                pltpu.make_async_copy(a.at[first:last], b.at[first:last], sems.at[n, i])
                for i, (a, b) in enumerate(pairs)
            ]
        )
        for i in (1, 0, 2):
            copies[n][i].start()
    first_key = (lax.axis_index("z") * 4 + lax.axis_index("y")) * SLICE
    draft = lax.broadcasted_iota(jnp.int32, (GROUP * DRAFTS, CHUNK), 0) % DRAFTS
    offset = draft - DRAFTS - lanes((GROUP * DRAFTS, CHUNK)) - first_key
    gain = gain_ref[...].astype(F32).reshape(1, 32)
    gain = jnp.concatenate([gain] * 4, axis=1).reshape(1, 1, HD)
    lane = lanes((GROUP, 8, HD))
    for row in range(ROWS):
        if row < 2:
            copies[row][0].wait()
        queries = jnp.concatenate(
            [q_ref[row, :, g * HD : (g + 1) * HD] for g in range(GROUP)], axis=0
        )
        limit = offset + lengths_ref[row]
        peak = jnp.full((GROUP * DRAFTS, HD), NEG, F32)
        if row < 2:
            copies[row][1].wait()
        for n in range(SLICE // CHUNK):
            scores = nt(queries, k_ref[row, n * CHUNK : (n + 1) * CHUNK, :]) * LOG_SCALE
            scores = jnp.where(limit >= n * CHUNK, scores, NEG)
            score_ref[row % 2, :, n * CHUNK : (n + 1) * CHUNK] = scores
            for i in range(CHUNK // HD):
                peak = jnp.maximum(peak, scores[:, i * HD : (i + 1) * HD])
        top = jnp.max(peak, axis=1, keepdims=True).astype(BF16).astype(F32)
        base = jnp.maximum(top, FLOOR)
        acc = jnp.zeros((GROUP * DRAFTS, HD), F32)
        sums = jnp.zeros((GROUP * DRAFTS, HD), F32)
        if row < 2:
            copies[row][2].wait()
        for n in range(SLICE // CHUNK):
            weights = jnp.exp2(score_ref[row % 2, :, n * CHUNK : (n + 1) * CHUNK] - base)
            for i in range(CHUNK // HD):
                sums = sums + weights[:, i * HD : (i + 1) * HD]
            acc = acc + nn(weights.astype(BF16), v_ref[row, n * CHUNK : (n + 1) * CHUNK, :])
        total = jnp.sum(sums, axis=1, keepdims=True).reshape(GROUP, DRAFTS, 1)
        top = top.reshape(GROUP, DRAFTS, 1)
        stats = jnp.where(lane < 64, total[:, 8:], gain)
        stats = jnp.where(lane < 48, total[:, :8], stats)
        stats = jnp.where(lane < 32, top[:, 8:], stats)
        stats = jnp.where(lane < 16, top[:, :8], stats)
        acc = acc.reshape(GROUP, DRAFTS, HD)
        block = jnp.concatenate([acc, stats], axis=1).astype(BF16)
        out_ref[row * GROUP : (row + 1) * GROUP] = block


def attention(lengths, gain, queries, keys, values):
    held = pl.BlockSpec(memory_space=pltpu.HBM)
    return pl.pallas_call(
        attend,
        in_specs=[SMEM, VMEM, held, held, held],
        out_specs=VMEM,
        out_shape=jax.ShapeDtypeStruct((KV, 24, HD), BF16),
        scratch_shapes=[
            pltpu.VMEM((ROWS, DRAFTS, GROUP * HD), BF16),
            pltpu.VMEM((ROWS, SLICE, HD), BF16),
            pltpu.VMEM((ROWS, SLICE, HD), BF16),
            pltpu.VMEM((2, GROUP * DRAFTS, SLICE), F32),
            pltpu.SemaphoreType.DMA((2, 3)),
        ],
        compiler_params=pltpu.CompilerParams(vmem_limit_bytes=57 * MIB),
        name="attention",
    )(lengths, gain, queries, keys, values)


def combine(in_ref, attn_ref, gain_ref):
    parts = in_ref[...].astype(F32)
    stats = parts[:, 16:24]
    top = jnp.concatenate([stats[:, :, 0:1], stats[:, :, 16:17]], axis=1)
    total = jnp.concatenate([stats[:, :, 32:33], stats[:, :, 48:49]], axis=1)
    joint = jnp.max(top, axis=0, keepdims=True)
    factor = jnp.exp2(top - joint)
    whole = jnp.sum(total * factor, axis=0)
    acc = jnp.sum(parts[:, 0:16] * factor, axis=0)
    attn = (acc / whole).astype(BF16)
    attn_ref[...] = jnp.broadcast_to(attn[None], (KV, DRAFTS, HD))
    pick = lanes((KV, KV * 8)) == 8 * lax.broadcasted_iota(jnp.int32, (KV, KV * 8), 0)
    stats = stats.reshape(KV * 8, HD).astype(BF16)
    gain_ref[...] = nn(pick.astype(F32).astype(BF16), stats).astype(BF16)


def combined(parts):
    return pl.pallas_call(
        combine,
        in_specs=[VMEM],
        out_specs=[VMEM, VMEM],
        out_shape=[
            jax.ShapeDtypeStruct((KV, DRAFTS, HD), BF16),
            jax.ShapeDtypeStruct((KV, HD), BF16),
        ],
        compiler_params=pltpu.CompilerParams(vmem_limit_bytes=16 * MIB),
        cost_estimate=pl.CostEstimate(
            flops=10000000000, bytes_accessed=0, transcendentals=0
        ),
        name="combine",
    )(parts)


def project(attn_ref, weight_ref, residual_ref, gain_ref, *refs):
    own_ref, other_ref = refs[-2:]
    head = lax.axis_index("x") * 2 + lax.axis_index("c")
    attn = jnp.concatenate(
        [
            jnp.concatenate([attn_ref[r * GROUP + g] for g in range(GROUP)], axis=1)
            for r in range(ROWS)
        ],
        axis=0,
    )
    spread = nn(attn, weight_ref[...])
    source = lax.broadcasted_iota(jnp.int32, (32, 256), 0)
    put = (lanes((32, 256)) == head * 32 + source).astype(F32).astype(BF16)
    spread = spread + tn(residual_ref[...], put)
    source = lax.broadcasted_iota(jnp.int32, (HD, 256), 0)
    put = (lanes((HD, 256)) == head * 32 + source - 64) & (source >= 64) & (source < 96)
    gain = nn(gain_ref[...], put.astype(F32).astype(BF16))
    both = jnp.concatenate([spread, gain], axis=0)
    core = lax.axis_index("c")
    own_ref[: TOKENS + KV] = jnp.where(core == 0, both[:, :HD], both[:, HD:])
    other_ref[: TOKENS + KV] = jnp.where(core == 0, both[:, HD:], both[:, :HD]).astype(BF16)
    spot = lanes((DRAFTS, HD)) // 32
    for half in range(2):
        part = spread[:, half * HD : (half + 1) * HD]
        rows = [part[a * DRAFTS : (a + 1) * DRAFTS] for a in range(4)]
        rows = [pltpu.roll(row, a * 32, 1) if a else row for a, row in enumerate(rows)]
        for i in range(0, 4, 2):
            tiles = []
            for j in (i, i + 1):
                tile = rows[0]
                for a in range(1, 4):
                    tile = jnp.where(spot == (j + a) % 4, rows[a], tile)
                tiles.append(tile)
            start = TOKENS + KV + (half * 2 + i // 2) * DRAFTS
            own_ref[start : start + DRAFTS] = jnp.where(core == 0, tiles[0], tiles[1])
            other_ref[start : start + DRAFTS] = jnp.where(core == 0, tiles[1], tiles[0]).astype(BF16)


def projected(attn, weight, residual, gain, held):
    return pl.pallas_call(
        project,
        in_specs=[VMEM] * 4 + [pl.BlockSpec(memory_space=pl.ANY)] * len(held),
        out_specs=[VMEM, VMEM],
        out_shape=[
            jax.ShapeDtypeStruct((TOKENS + KV + 4 * DRAFTS, HD), F32),
            jax.ShapeDtypeStruct((TOKENS + KV + 4 * DRAFTS, HD), BF16),
        ],
        compiler_params=pltpu.CompilerParams(vmem_limit_bytes=8 * MIB),
        cost_estimate=pl.CostEstimate(
            flops=1000000000, bytes_accessed=0, transcendentals=0
        ),
        name="project",
    )(attn, weight, residual, gain, *held)


def pair(own_ref, other_ref, *refs):
    sum_ref = refs[4]
    sum_ref[...] = own_ref[...] + other_ref[...].astype(F32)
    common = sum_ref[: TOKENS + KV].astype(BF16)
    for s in range(4):
        x = (lax.axis_index("x") + s) % 4
        start = pl.multiple_of(TOKENS + KV + x * DRAFTS, DRAFTS)
        refs[s][: TOKENS + KV] = common
        refs[s][TOKENS + KV :] = sum_ref[pl.ds(start, DRAFTS), :].astype(BF16)


def paired(own, other):
    shape = jax.ShapeDtypeStruct((TOKENS + KV + DRAFTS, HD), BF16)
    return pl.pallas_call(
        pair,
        in_specs=[VMEM, VMEM],
        out_specs=[VMEM] * 4,
        out_shape=[shape] * 4,
        scratch_shapes=[pltpu.VMEM((TOKENS + KV + 4 * DRAFTS, HD), F32)],
        compiler_params=pltpu.CompilerParams(vmem_limit_bytes=8 * MIB),
        name="pair",
    )(own, other)


def mix(*refs):
    parts = refs[:4]
    spread_ref, mixed_ref, gain_ref = refs[-3:]
    total = (parts[0][...].astype(F32) + parts[1][...].astype(F32)) + (
        parts[2][...].astype(F32) + parts[3][...].astype(F32)
    )
    spread_ref[...] = jnp.broadcast_to(total[:TOKENS].astype(BF16)[None], (KV, TOKENS, HD))
    gain_ref[...] = total[TOKENS : TOKENS + KV]
    mixed_ref[...] = total[TOKENS + KV :].astype(BF16)


def mixing(parts, held):
    return pl.pallas_call(
        mix,
        in_specs=[VMEM] * 4 + [pl.BlockSpec(memory_space=pl.ANY)] * len(held),
        out_specs=[VMEM, VMEM, VMEM],
        out_shape=[
            jax.ShapeDtypeStruct((KV, TOKENS, HD), BF16),
            jax.ShapeDtypeStruct((DRAFTS, HD), BF16),
            jax.ShapeDtypeStruct((KV, HD), F32),
        ],
        compiler_params=pltpu.CompilerParams(vmem_limit_bytes=8 * MIB),
        cost_estimate=pl.CostEstimate(
            flops=1000000000, bytes_accessed=0, transcendentals=0
        ),
        name="mix",
    )(*parts, *held)


def widen(mixed_ref, gain_ref, *refs):
    weight_refs, out_ref = refs[:4], refs[4]
    core = lax.axis_index("c")
    units = weight_refs[0].shape[0]
    squares = jnp.zeros((TOKENS, HD), F32)
    sums = [jnp.zeros((units, TOKENS), F32) for _ in weight_refs]
    for k in range(0, KV, 2):
        scaled, places = [], []
        for i in (k, k + 1):
            part = mixed_ref[i].astype(F32)
            squares = squares + part * part
            scaled.append((part * gain_ref[i : i + 1, :]).astype(BF16))
            places.append(pl.ds(pl.multiple_of(i * 256 + core * HD, HD), HD))
        scaled = jnp.concatenate(scaled, axis=1)
        for i, ref in enumerate(weight_refs):
            weight = jnp.concatenate([ref[:, at] for at in places], axis=1)
            sums[i] = sums[i] + nt(weight, scaled)
    square = jnp.sum(jnp.transpose(squares), axis=0, keepdims=True)
    square = jnp.broadcast_to(square, (8, TOKENS))
    own = jnp.concatenate([sums[0], sums[1], square], axis=0)
    other = jnp.concatenate([sums[2], sums[3], square], axis=0)
    out_ref[...] = jnp.concatenate([own, other], axis=1)


def widened(mixed, gain, weights):
    return pl.pallas_call(
        widen,
        in_specs=[VMEM] * 6,
        out_specs=VMEM,
        out_shape=jax.ShapeDtypeStruct((2 * weights[0].shape[0] + 8, HD), F32),
        compiler_params=pltpu.CompilerParams(vmem_limit_bytes=16 * MIB),
        name="widen",
    )(mixed, gain, *weights)


def narrow(mine_ref, theirs_ref, own_ref, other_ref, *out_refs):
    core = lax.axis_index("c")
    units = own_ref.shape[0]
    total = mine_ref[...] + pltpu.roll(theirs_ref[...], TOKENS, 1)
    scale = lax.rsqrt(total[2 * units : 2 * units + 1] / D + EPSILON)
    gate = total[:units] * scale
    upward = total[units : 2 * units] * scale
    hidden = jnp.transpose(gate / (1.0 + jnp.exp(-gate)) * upward)
    hidden = jnp.concatenate([hidden[:TOKENS], hidden[TOKENS:]], axis=1).astype(BF16)
    spot = lanes((DRAFTS, HD)) // 32
    masks = [spot == (core + i) % 4 for i in range(4)]
    here = [(lax.axis_index("x") + s) % 4 for s in range(4)]
    for k in range(KV):
        weight = jnp.concatenate(
            [ref[:, k * 256 : (k + 1) * 256] for ref in (own_ref, other_ref)], axis=0
        )
        terms = nn(hidden, weight)
        tiles = []
        for half in range(2):
            part = terms[:, half * HD : (half + 1) * HD]
            pair_tiles = [part[:DRAFTS], part[:DRAFTS]]
            for a in range(1, 4):
                rows = pltpu.roll(part[a * DRAFTS : (a + 1) * DRAFTS], a * 32, 1)
                for odd in range(2):
                    pair_tiles[odd] = jnp.where(masks[(2 * odd + a) % 4], rows, pair_tiles[odd])
            tiles.extend(pair_tiles)
        for s in range(4):
            low = jnp.where(here[s] == 0, tiles[0], tiles[1])
            high = jnp.where(here[s] == 2, tiles[2], tiles[3])
            out_refs[s][k] = jnp.where(here[s] < 2, low, high).astype(BF16)


def narrowed(mine, theirs, own, other):
    return pl.pallas_call(
        narrow,
        in_specs=[VMEM] * 4,
        out_specs=[VMEM] * 4,
        out_shape=[jax.ShapeDtypeStruct((KV, DRAFTS, HD), BF16)] * 4,
        compiler_params=pltpu.CompilerParams(vmem_limit_bytes=16 * MIB),
        name="narrow",
    )(mine, theirs, own, other)


def partial_sum(*refs):
    total = (refs[0][...].astype(F32) + refs[1][...].astype(F32)) + (
        refs[2][...].astype(F32) + refs[3][...].astype(F32)
    )
    refs[4][...] = total.astype(BF16)


def summed(parts):
    return pl.pallas_call(
        partial_sum,
        in_specs=[VMEM] * 4,
        out_specs=VMEM,
        out_shape=jax.ShapeDtypeStruct((KV, DRAFTS, HD), BF16),
        compiler_params=pltpu.CompilerParams(vmem_limit_bytes=8 * MIB),
        name="partial_sum",
    )(*parts)


def finish(parts_ref, mixed_ref, out_ref):
    total = parts_ref[0].astype(F32) + mixed_ref[...].astype(F32)
    for k in range(1, KV):
        total = total + parts_ref[k].astype(F32)
    shift = lax.axis_index("x") * 2 + lax.axis_index("c")
    total = pltpu.roll(total, (8 - shift) % 4 * 32, 1)
    tall = jnp.concatenate([pltpu.roll(total, (4 - a) % 4 * 32, 1) for a in range(4)], axis=0)
    out_ref[...] = jnp.transpose(tall)[:32].astype(BF16)


def finished(parts, mixed):
    return pl.pallas_call(
        finish,
        in_specs=[VMEM] * 2,
        out_specs=VMEM,
        out_shape=jax.ShapeDtypeStruct((32, TOKENS), BF16),
        compiler_params=pltpu.CompilerParams(vmem_limit_bytes=8 * MIB),
        name="finish",
    )(parts, mixed)


SWAP = [(0, 1), (1, 0)]


def trade(part):
    return lax.ppermute(part, "c", SWAP)


def around(parts):
    return [parts[0]] + [
        lax.ppermute(part, "x", [(i, (i + s) % 4) for i in range(4)])
        for s, part in enumerate(parts[1:], 1)
    ]


def exchange(parts, axes):
    return lax.all_to_all(parts, axes, 0, 0, tiled=True)


def shards(
    lengths,
    queries,
    cache_keys,
    cache_values,
    residual_in,
    out_weight,
    norm_gain,
    gate_weight,
    up_weight,
    down_weight,
):
    weights = [gate_weight.T, up_weight.T]
    parts = attention(lengths, norm_gain, queries, cache_keys, cache_values)
    parts, down_weight = lax.optimization_barrier((parts, down_weight))
    other_down = trade(down_weight)
    attn, gain = combined(exchange(parts, ("z", "y")))
    attn = exchange(attn, ("z", "y"))
    own, other = projected(attn, out_weight, residual_in.T, gain, [])
    parts = paired(own, trade(other))
    parts, weights = lax.optimization_barrier((parts, weights))
    weights = weights + [trade(weight) for weight in weights]
    spread, mixed, gain = mixing(around(parts), [])
    sums = widened(exchange(spread, ("z", "y")), gain, weights)
    terms = summed(around(narrowed(sums, trade(sums), down_weight, other_down)))
    return finished(exchange(terms, ("z", "y")), mixed).T


def solution(mesh):
    fine = Mesh(mesh.devices.reshape(8, 4, 4, 2), ("z", "y", "x", "c"))
    kvseq, head = ("z", "y"), ("x", "c")
    every = kvseq + head
    placed = (
        P(),
        P(None, None, head),
        P(None, kvseq, head),
        P(None, kvseq, head),
        P(None, every),
        P(head, kvseq),
        P(every),
        P(None, every),
        P(None, every),
        P(every, None),
    )
    return jax.shard_map(
        shards, mesh=fine, in_specs=placed, out_specs=P(None, every), check_vma=False
    )
```

```python
import math

import jax
import jax.numpy as jnp
from jax import lax
from jax.experimental import pallas as pl
from jax.experimental.pallas import tpu as pltpu
from jax.sharding import Mesh, PartitionSpec as P

D = 8192
FF = 28672
HD = 128
GROUP = 8
ROWS = 4
DRAFTS = 16
TOKENS = 64
KV = 32
SLICE = 2048
CHUNK = 512
NEG = -1e30
FLOOR = -1e29
EPSILON = 1e-05
LOG_SCALE = math.log2(math.e) / math.sqrt(HD)
MIB = 1024 * 1024
F32 = jnp.float32
BF16 = jnp.bfloat16
VMEM = pl.BlockSpec(memory_space=pltpu.VMEM)
SMEM = pl.BlockSpec(memory_space=pltpu.SMEM)


def nt(a, b):
    return lax.dot_general(a, b, (((1,), (1,)), ((), ())), preferred_element_type=F32)


def nn(a, b):
    return jnp.dot(a, b, preferred_element_type=F32)


def tn(a, b):
    return lax.dot_general(a, b, (((0,), (0,)), ((), ())), preferred_element_type=F32)


def lanes(shape):
    return lax.broadcasted_iota(jnp.int32, shape, len(shape) - 1)


def attend(
    lengths_ref, gain_ref, queries_ref, keys_ref, values_ref, out_ref,
    q_ref, k_ref, v_ref, score_ref, sems,
):
    copies = []
    pairs = [(queries_ref, q_ref), (keys_ref, k_ref), (values_ref, v_ref)]
    for n, (first, last) in enumerate([(0, 1), (1, ROWS)]):
        copies.append(
            [
                pltpu.make_async_copy(a.at[first:last], b.at[first:last], sems.at[n, i])
                for i, (a, b) in enumerate(pairs)
            ]
        )
        for i in (1, 0, 2):
            copies[n][i].start()
    first_key = (lax.axis_index("z") * 4 + lax.axis_index("y")) * SLICE
    draft = lax.broadcasted_iota(jnp.int32, (GROUP * DRAFTS, CHUNK), 0) % DRAFTS
    offset = draft - DRAFTS - lanes((GROUP * DRAFTS, CHUNK)) - first_key
    gain = gain_ref[...].astype(F32).reshape(1, 32)
    gain = jnp.concatenate([gain] * 4, axis=1).reshape(1, 1, HD)
    lane = lanes((GROUP, 8, HD))
    for row in range(ROWS):
        if row < 2:
            copies[row][0].wait()
        queries = jnp.concatenate(
            [q_ref[row, :, g * HD : (g + 1) * HD] for g in range(GROUP)], axis=0
        )
        limit = offset + lengths_ref[row]
        peak = jnp.full((GROUP * DRAFTS, HD), NEG, F32)
        if row < 2:
            copies[row][1].wait()
        for n in range(SLICE // CHUNK):
            scores = nt(queries, k_ref[row, n * CHUNK : (n + 1) * CHUNK, :]) * LOG_SCALE
            scores = jnp.where(limit >= n * CHUNK, scores, NEG)
            score_ref[row % 2, :, n * CHUNK : (n + 1) * CHUNK] = scores
            for i in range(CHUNK // HD):
                peak = jnp.maximum(peak, scores[:, i * HD : (i + 1) * HD])
        top = jnp.max(peak, axis=1, keepdims=True).astype(BF16).astype(F32)
        base = jnp.maximum(top, FLOOR)
        acc = jnp.zeros((GROUP * DRAFTS, HD), F32)
        sums = jnp.zeros((GROUP * DRAFTS, HD), F32)
        if row < 2:
            copies[row][2].wait()
        for n in range(SLICE // CHUNK):
            weights = jnp.exp2(score_ref[row % 2, :, n * CHUNK : (n + 1) * CHUNK] - base)
            for i in range(CHUNK // HD):
                sums = sums + weights[:, i * HD : (i + 1) * HD]
            acc = acc + nn(weights.astype(BF16), v_ref[row, n * CHUNK : (n + 1) * CHUNK, :])
        total = jnp.sum(sums, axis=1, keepdims=True).reshape(GROUP, DRAFTS, 1)
        top = top.reshape(GROUP, DRAFTS, 1)
        stats = jnp.where(lane < 64, total[:, 8:], gain)
        stats = jnp.where(lane < 48, total[:, :8], stats)
        stats = jnp.where(lane < 32, top[:, 8:], stats)
        stats = jnp.where(lane < 16, top[:, :8], stats)
        acc = acc.reshape(GROUP, DRAFTS, HD)
        block = jnp.concatenate([acc, stats], axis=1).astype(BF16)
        out_ref[row * GROUP : (row + 1) * GROUP] = block


def attention(lengths, gain, queries, keys, values):
    held = pl.BlockSpec(memory_space=pltpu.HBM)
    return pl.pallas_call(
        attend,
        in_specs=[SMEM, VMEM, held, held, held],
        out_specs=VMEM,
        out_shape=jax.ShapeDtypeStruct((KV, 24, HD), BF16),
        scratch_shapes=[
            pltpu.VMEM((ROWS, DRAFTS, GROUP * HD), BF16),
            pltpu.VMEM((ROWS, SLICE, HD), BF16),
            pltpu.VMEM((ROWS, SLICE, HD), BF16),
            pltpu.VMEM((2, GROUP * DRAFTS, SLICE), F32),
            pltpu.SemaphoreType.DMA((2, 3)),
        ],
        compiler_params=pltpu.CompilerParams(vmem_limit_bytes=61 * MIB),
        name="attention",
    )(lengths, gain, queries, keys, values)


def combine(in_ref, attn_ref, gain_ref):
    parts = in_ref[...].astype(F32)
    stats = parts[:, 16:24]
    top = jnp.concatenate([stats[:, :, 0:1], stats[:, :, 16:17]], axis=1)
    total = jnp.concatenate([stats[:, :, 32:33], stats[:, :, 48:49]], axis=1)
    joint = jnp.max(top, axis=0, keepdims=True)
    factor = jnp.exp2(top - joint)
    whole = jnp.sum(total * factor, axis=0)
    acc = jnp.sum(parts[:, 0:16] * factor, axis=0)
    attn = (acc / whole).astype(BF16)
    attn_ref[...] = jnp.broadcast_to(attn[None], (KV, DRAFTS, HD))
    pick = lanes((KV, KV * 8)) == 8 * lax.broadcasted_iota(jnp.int32, (KV, KV * 8), 0)
    stats = stats.reshape(KV * 8, HD).astype(BF16)
    gain_ref[...] = nn(pick.astype(F32).astype(BF16), stats).astype(BF16)


def combined(parts):
    return pl.pallas_call(
        combine,
        in_specs=[VMEM],
        out_specs=[VMEM, VMEM],
        out_shape=[
            jax.ShapeDtypeStruct((KV, DRAFTS, HD), BF16),
            jax.ShapeDtypeStruct((KV, HD), BF16),
        ],
        compiler_params=pltpu.CompilerParams(vmem_limit_bytes=16 * MIB),
        cost_estimate=pl.CostEstimate(
            flops=10000000000, bytes_accessed=0, transcendentals=0
        ),
        name="combine",
    )(parts)


def project(attn_ref, weight_ref, residual_ref, gain_ref, *refs):
    own_ref, other_ref = refs[-2:]
    head = lax.axis_index("x") * 2 + lax.axis_index("c")
    attn = jnp.concatenate(
        [
            jnp.concatenate([attn_ref[r * GROUP + g] for g in range(GROUP)], axis=1)
            for r in range(ROWS)
        ],
        axis=0,
    )
    spread = nn(attn, weight_ref[...])
    source = lax.broadcasted_iota(jnp.int32, (32, 256), 0)
    put = (lanes((32, 256)) == head * 32 + source).astype(F32).astype(BF16)
    spread = spread + tn(residual_ref[...], put)
    source = lax.broadcasted_iota(jnp.int32, (HD, 256), 0)
    put = (lanes((HD, 256)) == head * 32 + source - 64) & (source >= 64) & (source < 96)
    gain = nn(gain_ref[...], put.astype(F32).astype(BF16))
    both = jnp.concatenate([spread, gain], axis=0)
    core = lax.axis_index("c")
    own_ref[: TOKENS + KV] = jnp.where(core == 0, both[:, :HD], both[:, HD:])
    other_ref[: TOKENS + KV] = jnp.where(core == 0, both[:, HD:], both[:, :HD]).astype(BF16)
    spot = lanes((DRAFTS, HD)) // 32
    for half in range(2):
        part = spread[:, half * HD : (half + 1) * HD]
        rows = [part[a * DRAFTS : (a + 1) * DRAFTS] for a in range(4)]
        rows = [pltpu.roll(row, a * 32, 1) if a else row for a, row in enumerate(rows)]
        for i in range(0, 4, 2):
            tiles = []
            for j in (i, i + 1):
                tile = rows[0]
                for a in range(1, 4):
                    tile = jnp.where(spot == (j + a) % 4, rows[a], tile)
                tiles.append(tile)
            start = TOKENS + KV + (half * 2 + i // 2) * DRAFTS
            own_ref[start : start + DRAFTS] = jnp.where(core == 0, tiles[0], tiles[1])
            other_ref[start : start + DRAFTS] = jnp.where(core == 0, tiles[1], tiles[0]).astype(BF16)


def projected(attn, weight, residual, gain, held):
    return pl.pallas_call(
        project,
        in_specs=[VMEM] * 4 + [pl.BlockSpec(memory_space=pl.ANY)] * len(held),
        out_specs=[VMEM, VMEM],
        out_shape=[
            jax.ShapeDtypeStruct((TOKENS + KV + 4 * DRAFTS, HD), F32),
            jax.ShapeDtypeStruct((TOKENS + KV + 4 * DRAFTS, HD), BF16),
        ],
        compiler_params=pltpu.CompilerParams(vmem_limit_bytes=8 * MIB),
        cost_estimate=pl.CostEstimate(
            flops=1000000000, bytes_accessed=0, transcendentals=0
        ),
        name="project",
    )(attn, weight, residual, gain, *held)


def pair(own_ref, other_ref, *refs):
    sum_ref = refs[4]
    sum_ref[...] = own_ref[...] + other_ref[...].astype(F32)
    common = sum_ref[: TOKENS + KV].astype(BF16)
    for s in range(4):
        x = (lax.axis_index("x") + s) % 4
        start = pl.multiple_of(TOKENS + KV + x * DRAFTS, DRAFTS)
        refs[s][: TOKENS + KV] = common
        refs[s][TOKENS + KV :] = sum_ref[pl.ds(start, DRAFTS), :].astype(BF16)


def paired(own, other):
    shape = jax.ShapeDtypeStruct((TOKENS + KV + DRAFTS, HD), BF16)
    return pl.pallas_call(
        pair,
        in_specs=[VMEM, VMEM],
        out_specs=[VMEM] * 4,
        out_shape=[shape] * 4,
        scratch_shapes=[pltpu.VMEM((TOKENS + KV + 4 * DRAFTS, HD), F32)],
        compiler_params=pltpu.CompilerParams(vmem_limit_bytes=8 * MIB),
        name="pair",
    )(own, other)


def mix(*refs):
    parts = refs[:4]
    spread_ref, mixed_ref, gain_ref = refs[-3:]
    total = (parts[0][...].astype(F32) + parts[1][...].astype(F32)) + (
        parts[2][...].astype(F32) + parts[3][...].astype(F32)
    )
    spread_ref[...] = jnp.broadcast_to(total[:TOKENS].astype(BF16)[None], (KV, TOKENS, HD))
    gain_ref[...] = total[TOKENS : TOKENS + KV]
    mixed_ref[...] = total[TOKENS + KV :].astype(BF16)


def mixing(parts, held):
    return pl.pallas_call(
        mix,
        in_specs=[VMEM] * 4 + [pl.BlockSpec(memory_space=pl.ANY)] * len(held),
        out_specs=[VMEM, VMEM, VMEM],
        out_shape=[
            jax.ShapeDtypeStruct((KV, TOKENS, HD), BF16),
            jax.ShapeDtypeStruct((DRAFTS, HD), BF16),
            jax.ShapeDtypeStruct((KV, HD), F32),
        ],
        compiler_params=pltpu.CompilerParams(vmem_limit_bytes=8 * MIB),
        cost_estimate=pl.CostEstimate(
            flops=1000000000, bytes_accessed=0, transcendentals=0
        ),
        name="mix",
    )(*parts, *held)


def widen(mixed_ref, gain_ref, *refs):
    weight_refs, out_ref = refs[:4], refs[4]
    core = lax.axis_index("c")
    units = weight_refs[0].shape[0]
    squares = jnp.zeros((TOKENS, HD), F32)
    sums = [jnp.zeros((units, TOKENS), F32) for _ in weight_refs]
    for k in range(0, KV, 2):
        scaled, places = [], []
        for i in (k, k + 1):
            part = mixed_ref[i].astype(F32)
            squares = squares + part * part
            scaled.append((part * gain_ref[i : i + 1, :]).astype(BF16))
            places.append(pl.ds(pl.multiple_of(i * 256 + core * HD, HD), HD))
        scaled = jnp.concatenate(scaled, axis=1)
        for i, ref in enumerate(weight_refs):
            weight = jnp.concatenate([ref[:, at] for at in places], axis=1)
            sums[i] = sums[i] + nt(weight, scaled)
    square = jnp.sum(jnp.transpose(squares), axis=0, keepdims=True)
    square = jnp.broadcast_to(square, (8, TOKENS))
    own = jnp.concatenate([sums[0], sums[1], square], axis=0)
    other = jnp.concatenate([sums[2], sums[3], square], axis=0)
    out_ref[...] = jnp.concatenate([own, other], axis=1)


def widened(mixed, gain, weights):
    return pl.pallas_call(
        widen,
        in_specs=[VMEM] * 6,
        out_specs=VMEM,
        out_shape=jax.ShapeDtypeStruct((2 * weights[0].shape[0] + 8, HD), F32),
        compiler_params=pltpu.CompilerParams(vmem_limit_bytes=16 * MIB),
        name="widen",
    )(mixed, gain, *weights)


def narrow(mine_ref, theirs_ref, own_ref, other_ref, *out_refs):
    core = lax.axis_index("c")
    units = own_ref.shape[0]
    total = mine_ref[...] + pltpu.roll(theirs_ref[...], TOKENS, 1)
    scale = lax.rsqrt(total[2 * units : 2 * units + 1] / D + EPSILON)
    gate = total[:units] * scale
    upward = total[units : 2 * units] * scale
    hidden = jnp.transpose(gate / (1.0 + jnp.exp(-gate)) * upward)
    hidden = jnp.concatenate([hidden[:TOKENS], hidden[TOKENS:]], axis=1).astype(BF16)
    spot = lanes((DRAFTS, HD)) // 32
    masks = [spot == (core + i) % 4 for i in range(4)]
    here = [(lax.axis_index("x") + s) % 4 for s in range(4)]
    for k in range(KV):
        weight = jnp.concatenate(
            [ref[:, k * 256 : (k + 1) * 256] for ref in (own_ref, other_ref)], axis=0
        )
        terms = nn(hidden, weight)
        tiles = []
        for half in range(2):
            part = terms[:, half * HD : (half + 1) * HD]
            pair_tiles = [part[:DRAFTS], part[:DRAFTS]]
            for a in range(1, 4):
                rows = pltpu.roll(part[a * DRAFTS : (a + 1) * DRAFTS], a * 32, 1)
                for odd in range(2):
                    pair_tiles[odd] = jnp.where(masks[(2 * odd + a) % 4], rows, pair_tiles[odd])
            tiles.extend(pair_tiles)
        for s in range(4):
            low = jnp.where(here[s] == 0, tiles[0], tiles[1])
            high = jnp.where(here[s] == 2, tiles[2], tiles[3])
            out_refs[s][k] = jnp.where(here[s] < 2, low, high).astype(BF16)


def narrowed(mine, theirs, own, other):
    return pl.pallas_call(
        narrow,
        in_specs=[VMEM] * 4,
        out_specs=[VMEM] * 4,
        out_shape=[jax.ShapeDtypeStruct((KV, DRAFTS, HD), BF16)] * 4,
        compiler_params=pltpu.CompilerParams(vmem_limit_bytes=16 * MIB),
        name="narrow",
    )(mine, theirs, own, other)


def partial_sum(*refs):
    total = (refs[0][...].astype(F32) + refs[1][...].astype(F32)) + (
        refs[2][...].astype(F32) + refs[3][...].astype(F32)
    )
    refs[4][...] = total.astype(BF16)


def summed(parts):
    return pl.pallas_call(
        partial_sum,
        in_specs=[VMEM] * 4,
        out_specs=VMEM,
        out_shape=jax.ShapeDtypeStruct((KV, DRAFTS, HD), BF16),
        compiler_params=pltpu.CompilerParams(vmem_limit_bytes=8 * MIB),
        name="partial_sum",
    )(*parts)


def finish(parts_ref, mixed_ref, out_ref):
    total = parts_ref[0].astype(F32) + mixed_ref[...].astype(F32)
    for k in range(1, KV):
        total = total + parts_ref[k].astype(F32)
    shift = lax.axis_index("x") * 2 + lax.axis_index("c")
    total = pltpu.roll(total, (8 - shift) % 4 * 32, 1)
    tall = jnp.concatenate([pltpu.roll(total, (4 - a) % 4 * 32, 1) for a in range(4)], axis=0)
    out_ref[...] = jnp.transpose(tall)[:32].astype(BF16)


def finished(parts, mixed):
    return pl.pallas_call(
        finish,
        in_specs=[VMEM] * 2,
        out_specs=VMEM,
        out_shape=jax.ShapeDtypeStruct((32, TOKENS), BF16),
        compiler_params=pltpu.CompilerParams(vmem_limit_bytes=8 * MIB),
        name="finish",
    )(parts, mixed)


SWAP = [(0, 1), (1, 0)]


def trade(part):
    return lax.ppermute(part, "c", SWAP)


def around(parts):
    return [parts[0]] + [
        lax.ppermute(part, "x", [(i, (i + s) % 4) for i in range(4)])
        for s, part in enumerate(parts[1:], 1)
    ]


def exchange(parts, axes):
    return lax.all_to_all(parts, axes, 0, 0, tiled=True)


def shards(
    lengths,
    queries,
    cache_keys,
    cache_values,
    residual_in,
    out_weight,
    norm_gain,
    gate_weight,
    up_weight,
    down_weight,
):
    weights = [gate_weight.T, up_weight.T]
    parts = attention(lengths, norm_gain, queries, cache_keys, cache_values)
    parts, down_weight = lax.optimization_barrier((parts, down_weight))
    other_down = trade(down_weight)
    attn, gain = combined(exchange(parts, ("z", "y")))
    attn = exchange(attn, ("z", "y"))
    own, other = projected(attn, out_weight, residual_in.T, gain, [])
    parts = paired(own, trade(other))
    parts, weights = lax.optimization_barrier((parts, weights))
    weights = weights + [trade(weight) for weight in weights]
    spread, mixed, gain = mixing(around(parts), [])
    sums = widened(exchange(spread, ("z", "y")), gain, weights)
    terms = summed(around(narrowed(sums, trade(sums), down_weight, other_down)))
    return finished(exchange(terms, ("z", "y")), mixed).T


def solution(mesh):
    fine = Mesh(mesh.devices.reshape(8, 4, 4, 2), ("z", "y", "x", "c"))
    kvseq, head = ("z", "y"), ("x", "c")
    every = kvseq + head
    placed = (
        P(),
        P(None, None, head),
        P(None, kvseq, head),
        P(None, kvseq, head),
        P(None, every),
        P(head, kvseq),
        P(every),
        P(None, every),
        P(None, every),
        P(every, None),
    )
    return jax.shard_map(
        shards, mesh=fine, in_specs=placed, out_specs=P(None, every), check_vma=False
    )
```

```python
import math

import jax
import jax.numpy as jnp
from jax import lax
from jax.experimental import pallas as pl
from jax.experimental.pallas import tpu as pltpu
from jax.sharding import Mesh, PartitionSpec as P

D = 8192
FF = 28672
HD = 128
GROUP = 8
ROWS = 4
DRAFTS = 16
TOKENS = 64
KV = 32
SLICE = 2048
CHUNK = 512
NEG = -1e30
FLOOR = -1e29
EPSILON = 1e-05
LOG_SCALE = math.log2(math.e) / math.sqrt(HD)
MIB = 1024 * 1024
F32 = jnp.float32
BF16 = jnp.bfloat16
VMEM = pl.BlockSpec(memory_space=pltpu.VMEM)
SMEM = pl.BlockSpec(memory_space=pltpu.SMEM)


def nt(a, b):
    return lax.dot_general(a, b, (((1,), (1,)), ((), ())), preferred_element_type=F32)


def nn(a, b):
    return jnp.dot(a, b, preferred_element_type=F32)


def tn(a, b):
    return lax.dot_general(a, b, (((0,), (0,)), ((), ())), preferred_element_type=F32)


def lanes(shape):
    return lax.broadcasted_iota(jnp.int32, shape, len(shape) - 1)


def attend(
    lengths_ref, gain_ref, queries_ref, keys_ref, values_ref, out_ref,
    q_ref, k_ref, v_ref, score_ref, sems,
):
    copies = []
    pairs = [(queries_ref, q_ref), (keys_ref, k_ref), (values_ref, v_ref)]
    for n, (first, last) in enumerate([(0, 1), (1, ROWS)]):
        copies.append(
            [
                pltpu.make_async_copy(a.at[first:last], b.at[first:last], sems.at[n, i])
                for i, (a, b) in enumerate(pairs)
            ]
        )
        for i in (1, 0, 2):
            copies[n][i].start()
    first_key = (lax.axis_index("z") * 4 + lax.axis_index("y")) * SLICE
    draft = lax.broadcasted_iota(jnp.int32, (GROUP * DRAFTS, CHUNK), 0) % DRAFTS
    offset = draft - DRAFTS - lanes((GROUP * DRAFTS, CHUNK)) - first_key
    gain = gain_ref[...].astype(F32).reshape(1, 32)
    gain = jnp.concatenate([gain] * 4, axis=1).reshape(1, 1, HD)
    lane = lanes((GROUP, 8, HD))
    for row in range(ROWS):
        if row < 2:
            copies[row][0].wait()
        queries = jnp.concatenate(
            [q_ref[row, :, g * HD : (g + 1) * HD] for g in range(GROUP)], axis=0
        )
        limit = offset + lengths_ref[row]
        peak = jnp.full((GROUP * DRAFTS, HD), NEG, F32)
        if row < 2:
            copies[row][1].wait()
        for n in range(SLICE // CHUNK):
            scores = nt(queries, k_ref[row, n * CHUNK : (n + 1) * CHUNK, :]) * LOG_SCALE
            scores = jnp.where(limit >= n * CHUNK, scores, NEG)
            score_ref[row % 2, :, n * CHUNK : (n + 1) * CHUNK] = scores
            for i in range(CHUNK // HD):
                peak = jnp.maximum(peak, scores[:, i * HD : (i + 1) * HD])
        top = jnp.max(peak, axis=1, keepdims=True).astype(BF16).astype(F32)
        base = jnp.maximum(top, FLOOR)
        acc = jnp.zeros((GROUP * DRAFTS, HD), F32)
        sums = jnp.zeros((GROUP * DRAFTS, HD), F32)
        if row < 2:
            copies[row][2].wait()
        for n in range(SLICE // CHUNK):
            weights = jnp.exp2(score_ref[row % 2, :, n * CHUNK : (n + 1) * CHUNK] - base)
            for i in range(CHUNK // HD):
                sums = sums + weights[:, i * HD : (i + 1) * HD]
            acc = acc + nn(weights.astype(BF16), v_ref[row, n * CHUNK : (n + 1) * CHUNK, :])
        total = jnp.sum(sums, axis=1, keepdims=True).reshape(GROUP, DRAFTS, 1)
        top = top.reshape(GROUP, DRAFTS, 1)
        stats = jnp.where(lane < 64, total[:, 8:], gain)
        stats = jnp.where(lane < 48, total[:, :8], stats)
        stats = jnp.where(lane < 32, top[:, 8:], stats)
        stats = jnp.where(lane < 16, top[:, :8], stats)
        acc = acc.reshape(GROUP, DRAFTS, HD)
        block = jnp.concatenate([acc, stats], axis=1).astype(BF16)
        out_ref[row * GROUP : (row + 1) * GROUP] = block


def attention(lengths, gain, queries, keys, values):
    held = pl.BlockSpec(memory_space=pltpu.HBM)
    return pl.pallas_call(
        attend,
        in_specs=[SMEM, VMEM, held, held, held],
        out_specs=VMEM,
        out_shape=jax.ShapeDtypeStruct((KV, 24, HD), BF16),
        scratch_shapes=[
            pltpu.VMEM((ROWS, DRAFTS, GROUP * HD), BF16),
            pltpu.VMEM((ROWS, SLICE, HD), BF16),
            pltpu.VMEM((ROWS, SLICE, HD), BF16),
            pltpu.VMEM((2, GROUP * DRAFTS, SLICE), F32),
            pltpu.SemaphoreType.DMA((2, 3)),
        ],
        compiler_params=pltpu.CompilerParams(vmem_limit_bytes=57 * MIB),
        name="attention",
    )(lengths, gain, queries, keys, values)


def combine(in_ref, attn_ref, gain_ref):
    parts = in_ref[...].astype(F32)
    stats = parts[:, 16:24]
    top = jnp.concatenate([stats[:, :, 0:1], stats[:, :, 16:17]], axis=1)
    total = jnp.concatenate([stats[:, :, 32:33], stats[:, :, 48:49]], axis=1)
    joint = jnp.max(top, axis=0, keepdims=True)
    factor = jnp.exp2(top - joint)
    whole = jnp.sum(total * factor, axis=0)
    acc = jnp.sum(parts[:, 0:16] * factor, axis=0)
    attn = (acc / whole).astype(BF16)
    attn_ref[...] = jnp.broadcast_to(attn[None], (KV, DRAFTS, HD))
    pick = lanes((KV, KV * 8)) == 8 * lax.broadcasted_iota(jnp.int32, (KV, KV * 8), 0)
    stats = stats.reshape(KV * 8, HD).astype(BF16)
    gain_ref[...] = nn(pick.astype(F32).astype(BF16), stats).astype(BF16)


def combined(parts):
    return pl.pallas_call(
        combine,
        in_specs=[VMEM],
        out_specs=[VMEM, VMEM],
        out_shape=[
            jax.ShapeDtypeStruct((KV, DRAFTS, HD), BF16),
            jax.ShapeDtypeStruct((KV, HD), BF16),
        ],
        compiler_params=pltpu.CompilerParams(vmem_limit_bytes=16 * MIB),
        cost_estimate=pl.CostEstimate(
            flops=10000000000, bytes_accessed=0, transcendentals=0
        ),
        name="combine",
    )(parts)


def project(attn_ref, weight_ref, residual_ref, gain_ref, *refs):
    own_ref, other_ref = refs[-2:]
    head = lax.axis_index("x") * 2 + lax.axis_index("c")
    attn = jnp.concatenate(
        [
            jnp.concatenate([attn_ref[r * GROUP + g] for g in range(GROUP)], axis=1)
            for r in range(ROWS)
        ],
        axis=0,
    )
    spread = nn(attn, weight_ref[...])
    source = lax.broadcasted_iota(jnp.int32, (32, 256), 0)
    put = (lanes((32, 256)) == head * 32 + source).astype(F32).astype(BF16)
    spread = spread + tn(residual_ref[...], put)
    source = lax.broadcasted_iota(jnp.int32, (HD, 256), 0)
    put = (lanes((HD, 256)) == head * 32 + source - 64) & (source >= 64) & (source < 96)
    gain = nn(gain_ref[...], put.astype(F32).astype(BF16))
    both = jnp.concatenate([spread, gain], axis=0)
    core = lax.axis_index("c")
    own_ref[: TOKENS + KV] = jnp.where(core == 0, both[:, :HD], both[:, HD:])
    other_ref[: TOKENS + KV] = jnp.where(core == 0, both[:, HD:], both[:, :HD]).astype(BF16)
    spot = lanes((DRAFTS, HD)) // 32
    for half in range(2):
        part = spread[:, half * HD : (half + 1) * HD]
        rows = [part[a * DRAFTS : (a + 1) * DRAFTS] for a in range(4)]
        rows = [pltpu.roll(row, a * 32, 1) if a else row for a, row in enumerate(rows)]
        for i in range(0, 4, 2):
            tiles = []
            for j in (i, i + 1):
                tile = rows[0]
                for a in range(1, 4):
                    tile = jnp.where(spot == (j + a) % 4, rows[a], tile)
                tiles.append(tile)
            start = TOKENS + KV + (half * 2 + i // 2) * DRAFTS
            own_ref[start : start + DRAFTS] = jnp.where(core == 0, tiles[0], tiles[1])
            other_ref[start : start + DRAFTS] = jnp.where(core == 0, tiles[1], tiles[0]).astype(BF16)


def projected(attn, weight, residual, gain, held):
    return pl.pallas_call(
        project,
        in_specs=[VMEM] * 4 + [pl.BlockSpec(memory_space=pl.ANY)] * len(held),
        out_specs=[VMEM, VMEM],
        out_shape=[
            jax.ShapeDtypeStruct((TOKENS + KV + 4 * DRAFTS, HD), F32),
            jax.ShapeDtypeStruct((TOKENS + KV + 4 * DRAFTS, HD), BF16),
        ],
        compiler_params=pltpu.CompilerParams(vmem_limit_bytes=8 * MIB),
        cost_estimate=pl.CostEstimate(
            flops=1000000000, bytes_accessed=0, transcendentals=0
        ),
        name="project",
    )(attn, weight, residual, gain, *held)


def pair(own_ref, other_ref, *refs):
    sum_ref = refs[4]
    sum_ref[...] = own_ref[...] + other_ref[...].astype(F32)
    common = sum_ref[: TOKENS + KV].astype(BF16)
    for s in range(4):
        x = (lax.axis_index("x") + s) % 4
        start = pl.multiple_of(TOKENS + KV + x * DRAFTS, DRAFTS)
        refs[s][: TOKENS + KV] = common
        refs[s][TOKENS + KV :] = sum_ref[pl.ds(start, DRAFTS), :].astype(BF16)


def paired(own, other):
    shape = jax.ShapeDtypeStruct((TOKENS + KV + DRAFTS, HD), BF16)
    return pl.pallas_call(
        pair,
        in_specs=[VMEM, VMEM],
        out_specs=[VMEM] * 4,
        out_shape=[shape] * 4,
        scratch_shapes=[pltpu.VMEM((TOKENS + KV + 4 * DRAFTS, HD), F32)],
        compiler_params=pltpu.CompilerParams(vmem_limit_bytes=8 * MIB),
        name="pair",
    )(own, other)


def mix(*refs):
    parts = refs[:4]
    spread_ref, mixed_ref, gain_ref = refs[-3:]
    total = (parts[0][...].astype(F32) + parts[1][...].astype(F32)) + (
        parts[2][...].astype(F32) + parts[3][...].astype(F32)
    )
    spread_ref[...] = jnp.broadcast_to(total[:TOKENS].astype(BF16)[None], (KV, TOKENS, HD))
    gain_ref[...] = total[TOKENS : TOKENS + KV]
    mixed_ref[...] = total[TOKENS + KV :].astype(BF16)


def mixing(parts, held):
    return pl.pallas_call(
        mix,
        in_specs=[VMEM] * 4 + [pl.BlockSpec(memory_space=pl.ANY)] * len(held),
        out_specs=[VMEM, VMEM, VMEM],
        out_shape=[
            jax.ShapeDtypeStruct((KV, TOKENS, HD), BF16),
            jax.ShapeDtypeStruct((DRAFTS, HD), BF16),
            jax.ShapeDtypeStruct((KV, HD), F32),
        ],
        compiler_params=pltpu.CompilerParams(vmem_limit_bytes=8 * MIB),
        cost_estimate=pl.CostEstimate(
            flops=1000000000, bytes_accessed=0, transcendentals=0
        ),
        name="mix",
    )(*parts, *held)


def widen(mixed_ref, gain_ref, *refs):
    weight_refs, out_ref = refs[:4], refs[4]
    core = lax.axis_index("c")
    units = weight_refs[0].shape[0]
    squares = jnp.zeros((TOKENS, HD), F32)
    sums = [jnp.zeros((units, TOKENS), F32) for _ in weight_refs]
    for k in range(0, KV, 2):
        scaled, places = [], []
        for i in (k, k + 1):
            part = mixed_ref[i].astype(F32)
            squares = squares + part * part
            scaled.append((part * gain_ref[i : i + 1, :]).astype(BF16))
            places.append(pl.ds(pl.multiple_of(i * 256 + core * HD, HD), HD))
        scaled = jnp.concatenate(scaled, axis=1)
        for i, ref in enumerate(weight_refs):
            weight = jnp.concatenate([ref[:, at] for at in places], axis=1)
            sums[i] = sums[i] + nt(weight, scaled)
    square = jnp.sum(jnp.transpose(squares), axis=0, keepdims=True)
    square = jnp.broadcast_to(square, (8, TOKENS))
    own = jnp.concatenate([sums[0], sums[1], square], axis=0)
    other = jnp.concatenate([sums[2], sums[3], square], axis=0)
    out_ref[...] = jnp.concatenate([own, other], axis=1)


def widened(mixed, gain, weights):
    return pl.pallas_call(
        widen,
        in_specs=[VMEM] * 6,
        out_specs=VMEM,
        out_shape=jax.ShapeDtypeStruct((2 * weights[0].shape[0] + 8, HD), F32),
        compiler_params=pltpu.CompilerParams(vmem_limit_bytes=16 * MIB),
        name="widen",
    )(mixed, gain, *weights)


def narrow(mine_ref, theirs_ref, own_ref, other_ref, *out_refs):
    core = lax.axis_index("c")
    units = own_ref.shape[0]
    total = mine_ref[...] + pltpu.roll(theirs_ref[...], TOKENS, 1)
    scale = lax.rsqrt(total[2 * units : 2 * units + 1] / D + EPSILON)
    gate = total[:units] * scale
    upward = total[units : 2 * units] * scale
    hidden = jnp.transpose(gate / (1.0 + jnp.exp(-gate)) * upward)
    hidden = jnp.concatenate([hidden[:TOKENS], hidden[TOKENS:]], axis=1).astype(BF16)
    spot = lanes((DRAFTS, HD)) // 32
    masks = [spot == (core + i) % 4 for i in range(4)]
    for n in range(KV):
        y = (lax.axis_index("y") + n // 8) % 4
        at = pl.ds(pl.multiple_of((n % 8 * 4 + y) * 256, 256), 256)
        weight = jnp.concatenate([ref[:, at] for ref in (own_ref, other_ref)], axis=0)
        terms = nn(hidden, weight)
        tiles = []
        for half in range(2):
            part = terms[:, half * HD : (half + 1) * HD]
            pair_tiles = [part[:DRAFTS], part[:DRAFTS]]
            for a in range(1, 4):
                rows = pltpu.roll(part[a * DRAFTS : (a + 1) * DRAFTS], a * 32, 1)
                for odd in range(2):
                    pair_tiles[odd] = jnp.where(masks[(2 * odd + a) % 4], rows, pair_tiles[odd])
            tiles.extend(pair_tiles)
        for x in range(4):
            out_refs[n // 8][n % 8 * 4 + x] = tiles[x].astype(BF16)


def narrowed(mine, theirs, own, other):
    return pl.pallas_call(
        narrow,
        in_specs=[VMEM] * 4,
        out_specs=[VMEM] * 4,
        out_shape=[jax.ShapeDtypeStruct((KV, DRAFTS, HD), BF16)] * 4,
        compiler_params=pltpu.CompilerParams(vmem_limit_bytes=16 * MIB),
        name="narrow",
    )(mine, theirs, own, other)


def partial_sum(*refs):
    total = (refs[0][...].astype(F32) + refs[1][...].astype(F32)) + (
        refs[2][...].astype(F32) + refs[3][...].astype(F32)
    )
    refs[4][...] = total.astype(BF16)


def summed(parts):
    return pl.pallas_call(
        partial_sum,
        in_specs=[VMEM] * 4,
        out_specs=VMEM,
        out_shape=jax.ShapeDtypeStruct((KV, DRAFTS, HD), BF16),
        compiler_params=pltpu.CompilerParams(vmem_limit_bytes=8 * MIB),
        name="partial_sum",
    )(*parts)


def finish(parts_ref, mixed_ref, out_ref):
    total = parts_ref[0].astype(F32) + mixed_ref[...].astype(F32)
    for k in range(1, KV):
        total = total + parts_ref[k].astype(F32)
    shift = lax.axis_index("x") * 2 + lax.axis_index("c")
    total = pltpu.roll(total, (8 - shift) % 4 * 32, 1)
    tall = jnp.concatenate([pltpu.roll(total, (4 - a) % 4 * 32, 1) for a in range(4)], axis=0)
    out_ref[...] = jnp.transpose(tall)[:32].astype(BF16)


def finished(parts, mixed):
    return pl.pallas_call(
        finish,
        in_specs=[VMEM] * 2,
        out_specs=VMEM,
        out_shape=jax.ShapeDtypeStruct((32, TOKENS), BF16),
        compiler_params=pltpu.CompilerParams(vmem_limit_bytes=8 * MIB),
        name="finish",
    )(parts, mixed)


SWAP = [(0, 1), (1, 0)]


def trade(part):
    return lax.ppermute(part, "c", SWAP)


def around(parts, axis):
    return [parts[0]] + [
        lax.ppermute(part, axis, [(i, (i + s) % 4) for i in range(4)])
        for s, part in enumerate(parts[1:], 1)
    ]


def exchange(parts, axes):
    return lax.all_to_all(parts, axes, 0, 0, tiled=True)


def shards(
    lengths,
    queries,
    cache_keys,
    cache_values,
    residual_in,
    out_weight,
    norm_gain,
    gate_weight,
    up_weight,
    down_weight,
):
    weights = [gate_weight.T, up_weight.T]
    parts = attention(lengths, norm_gain, queries, cache_keys, cache_values)
    parts, down_weight = lax.optimization_barrier((parts, down_weight))
    other_down = trade(down_weight)
    attn, gain = combined(exchange(parts, ("z", "y")))
    attn = exchange(attn, ("z", "y"))
    own, other = projected(attn, out_weight, residual_in.T, gain, [])
    parts = paired(own, trade(other))
    parts, weights = lax.optimization_barrier((parts, weights))
    weights = weights + [trade(weight) for weight in weights]
    spread, mixed, gain = mixing(around(parts, "x"), [])
    sums = widened(exchange(spread, ("z", "y")), gain, weights)
    terms = summed(around(narrowed(sums, trade(sums), down_weight, other_down), "y"))
    return finished(exchange(terms, ("z", "x")), mixed).T


def solution(mesh):
    fine = Mesh(mesh.devices.reshape(8, 4, 4, 2), ("z", "y", "x", "c"))
    kvseq, head = ("z", "y"), ("x", "c")
    every = kvseq + head
    placed = (
        P(),
        P(None, None, head),
        P(None, kvseq, head),
        P(None, kvseq, head),
        P(None, every),
        P(head, kvseq),
        P(every),
        P(None, every),
        P(None, every),
        P(every, None),
    )
    return jax.shard_map(
        shards, mesh=fine, in_specs=placed, out_specs=P(None, every), check_vma=False
    )
```
